128 devices in a mesh: head: 4 (over y), seq: 32 (over z, x, core).
Axes of the slice: x: 4, y: 4, z: 4, core: 2. Of those that a mesh axis runs over, the one named last changes fastest.
Arguments:
- inputs: bfloat16 [32768, 4096], P(('seq', 'head')), may hold values from -6 to 6
- dt_raw: bfloat16 [32768, 64], P(('seq', 'head')), may hold values from -4 to 4
- b_proj: bfloat16 [32768, 128], P(('seq', 'head')), may hold values from -0.59765625 to 0.59765625
- c_proj: bfloat16 [32768, 128], P(('seq', 'head')), may hold values from -0.59765625 to 0.59765625
- a_log: float32 [64], P('head'), may hold values from -12 to -2
- d_skip: float32 [64], P('head'), may hold values from 0.5 to 1.5
- seg_ids: int32 [32768], P('seq'), may hold values from 0 to 7, as said below
- cotangent: bfloat16 [32768, 4096], P(('seq', 'head')), may hold values from -6 to 6
Outputs:
- mixer_out: bfloat16 [32768, 4096], P(('seq', 'head'))
- grad_inputs: bfloat16 [32768, 4096], P(('seq', 'head'))
- grad_dt_raw: bfloat16 [32768, 64], P(('seq', 'head'))
- grad_b: float32 [32768, 128], P(('seq', 'head'))
- grad_c: float32 [32768, 128], P(('seq', 'head'))
- grad_a_log: float32 [64], P('head')
- grad_d_skip: float32 [64], P('head')
The draws below stay inside these ranges and needn't reach their ends.
Inputs may be any that keep to these rules, and one draw needn't show every extreme that they name: `seg_ids`: segment numbers never fall along the ordering and each is used; each segment is a contiguous run of at most 8192 tokens; segment 0 ends within the first 512 tokens and segment 1 has exactly 8192 tokens.
All inputs are finite; a program needn't handle non-finite values.
Results may differ from the reference program's by a relative error of at most 0.018.
Values may be sent and summed in bfloat16 or wider, within the bound.
No kernel may reach another device: no remote copies, remote signals or barrier semaphores. Data moves between devices by JAX's collectives and lax.ppermute only.
A program may use at most 256 MiB of HBM per device.

```python
import jax
import jax.numpy as jnp
from jax import lax

HEADS = 64
HEAD_DIM = 64
STATE = 128
BLOCK = 256
TOK_DEV = 1024
TOKENS = 32768


def draw_a_log(key, part):
    key = jax.random.fold_in(key, 11)
    lowest = jnp.log(0.5 / TOKENS)
    highest = jnp.log(1.0 / 16.0)
    return jax.random.uniform(key, (HEADS,), jnp.float32, lowest, highest)


def draw_seg_ids(key, part):
    key = jax.random.fold_in(key, 23)
    first_key, break_key = jax.random.split(key)
    head_len = jax.random.randint(first_key, (), 1, TOK_DEV // 2 + 1).astype(jnp.int32)
    positions = jnp.arange(TOKENS, dtype=jnp.int32)
    quarter = TOKENS // 4
    stride = TOKENS // 8
    base = quarter + TOK_DEV // 2
    count = (TOKENS - 1 - base) // stride
    long_end = head_len + quarter
    offsets = jax.random.randint(break_key, (count,), 1, stride + 1).astype(jnp.int32)
    break_pos = base + jnp.arange(count, dtype=jnp.int32) * stride + offsets
    passed = positions[:, None] >= break_pos[None, :]
    counted = jnp.sum(passed.astype(jnp.int32), axis=1)
    later = 2 + counted
    return jnp.where(positions < head_len, 0, jnp.where(positions < long_end, 1, later)).astype(jnp.int32)


def shard_levels(stream_key, extent, cuts, least, high):
    loudness, own = 1.0, jax.random.fold_in(stream_key, 6)
    for position, parts in cuts:
        heights = jnp.exp(jax.random.uniform(jax.random.fold_in(own, position), (parts,), jnp.float32, least / len(cuts), high / len(cuts)))
        loudness = loudness * jnp.repeat(heights, extent[position] // parts).reshape([-1 if axis == position else 1 for axis in range(len(extent))])
    return loudness


def centred(rng, shape, width, reach, pieces=(), held_as=jnp.bfloat16):
    entries = width * jax.random.normal(rng, shape, jnp.float32)
    if pieces:
        entries = entries * shard_levels(rng, shape, pieces, -0.22, 0.18)
    return jnp.clip(entries, -reach, reach).astype(held_as)


def setup_inputs(seed: int = 0) -> dict:
    seeds = jax.random.split(jax.random.key(seed), 9)
    inputs = centred(seeds[0], (TOKENS, HEADS * HEAD_DIM), 1.0, 6.0, ((0, 128),))
    dt_raw = centred(seeds[1], (TOKENS, HEADS), 1.0, 4.0, ((0, 128),))
    b_proj = centred(seeds[2], (TOKENS, STATE), 0.1, 0.59765625, ((0, 128),))
    c_proj = centred(seeds[3], (TOKENS, STATE), 0.1, 0.59765625, ((0, 128),))
    a_log = draw_a_log(jax.random.fold_in(seeds[8], 71), 0)
    d_skip = jnp.clip(0.5 + 1.0 * jax.random.uniform(seeds[5], (HEADS,), jnp.float32) ** shard_levels(seeds[5], (HEADS,), ((0, 4),), -0.2, 0.2), 0.5, 1.5)
    seg_ids = draw_seg_ids(jax.random.fold_in(seeds[8], 71), 0)
    cotangent = centred(seeds[7], (TOKENS, HEADS * HEAD_DIM), 1.0, 6.0, ((0, 128),))
    return dict(inputs=inputs, dt_raw=dt_raw, b_proj=b_proj, c_proj=c_proj, a_log=a_log, d_skip=d_skip, seg_ids=seg_ids, cotangent=cotangent)


def to_low(value):
    return lax.optimization_barrier(value.astype(jnp.bfloat16)).astype(jnp.float32)


def local_terms(x_blk, b_blk, c_blk, raw_blk, seg_blk, seg_before, decay_rate):
    dt_val = jax.nn.softplus(raw_blk.astype(jnp.float32))
    cum_log = jnp.cumsum(-decay_rate[None, :] * dt_val, axis=0)
    total_log = cum_log[-1]
    size_q = seg_blk.shape[0]
    row_pos = lax.broadcasted_iota(jnp.int32, (size_q, size_q), 0)
    col_pos = lax.broadcasted_iota(jnp.int32, (size_q, size_q), 1)
    keep_mask = ((seg_blk[:, None] == seg_blk[None, :]) & (row_pos >= col_pos))[:, :, None]
    log_gaps = cum_log[:, None, :] - cum_log[None, :, :]
    kern_decay = jnp.where(keep_mask, jnp.exp(jnp.where(keep_mask, log_gaps, 0.0)), 0.0)
    kern_full = kern_decay * dt_val[None, :, :]
    gram_block = jnp.dot(c_blk, b_blk.T, preferred_element_type=jnp.float32)
    mixed_terms = gram_block[:, :, None] * kern_full
    enter_gate = (seg_blk == seg_before).astype(jnp.float32)
    leave_gate = (seg_blk == seg_blk[-1]).astype(jnp.float32)
    end_decay = jnp.exp(total_log[None, :] - cum_log) * leave_gate[:, None]
    weight = end_decay * dt_val
    b_weighted = to_low(b_blk.astype(jnp.float32)[:, None, :] * weight[:, :, None])
    block_decay = jnp.exp(total_log) * enter_gate[-1]
    start_decay = jnp.exp(cum_log) * enter_gate[:, None]
    return dt_val, gram_block, kern_decay, kern_full, mixed_terms, end_decay, weight, b_weighted, block_decay, start_decay


def reference(inputs, dt_raw, b_proj, c_proj, a_log, d_skip, seg_ids, cotangent):
    blocks = TOKENS // BLOCK
    x_blocks = inputs.reshape(blocks, BLOCK, HEADS, HEAD_DIM)
    g_blocks = cotangent.reshape(blocks, BLOCK, HEADS, HEAD_DIM)
    raw_blocks = dt_raw.reshape(blocks, BLOCK, HEADS)
    b_blocks = b_proj.reshape(blocks, BLOCK, STATE)
    c_blocks = c_proj.reshape(blocks, BLOCK, STATE)
    seg_blocks = seg_ids.reshape(blocks, BLOCK)
    seg_prior = jnp.concatenate([jnp.zeros((1,), jnp.int32), seg_blocks[:-1, -1]])
    decay_rate = jnp.exp(a_log)
    zero_state = jnp.zeros((HEADS, STATE, HEAD_DIM), jnp.float32)

    def forward_step(h_prev, block_items):
        x_blk, b_blk, c_blk, raw_blk, seg_blk, seg_before = block_items
        terms = local_terms(x_blk, b_blk, c_blk, raw_blk, seg_blk, seg_before, decay_rate)
        mixed_terms, b_weighted, block_decay, start_decay = terms[4], terms[7], terms[8], terms[9]
        x_float = x_blk.astype(jnp.float32)
        mix_part = jnp.einsum("tsh,shp->thp", to_low(mixed_terms), x_float)
        contrib = jnp.einsum("shn,shp->hnp", b_weighted, x_float)
        h_low = to_low(h_prev)
        from_state = jnp.einsum("tn,hnp->thp", c_blk.astype(jnp.float32), h_low)
        y_blk = (mix_part + start_decay[:, :, None] * from_state + d_skip[None, :, None] * x_float).astype(jnp.bfloat16)
        h_next = block_decay[:, None, None] * h_prev + contrib
        return h_next, (y_blk, h_prev)

    _, (y_all, h_all) = lax.scan(forward_step, zero_state, (x_blocks, b_blocks, c_blocks, raw_blocks, seg_blocks, seg_prior))

    def backward_step(lam_state, block_items):
        x_blk, g_blk, b_blk, c_blk, raw_blk, seg_blk, seg_before, h_prev = block_items
        (dt_val, gram_block, kern_decay, kern_full, mixed_terms, end_decay, weight, b_weighted, block_decay, start_decay) = local_terms(
            x_blk, b_blk, c_blk, raw_blk, seg_blk, seg_before, decay_rate)
        x_float = x_blk.astype(jnp.float32)
        g_float = g_blk.astype(jnp.float32)
        b_float = b_blk.astype(jnp.float32)
        c_float = c_blk.astype(jnp.float32)
        h_low = to_low(h_prev)
        from_state = jnp.einsum("tn,hnp->thp", c_float, h_low)
        skip_grad = jnp.sum(g_float * x_float, axis=(0, 2))
        d_mix = jnp.einsum("thp,shp->tsh", g_float, x_float)
        dx_mix = jnp.einsum("tsh,thp->shp", to_low(mixed_terms), g_float)
        prod_terms = d_mix * mixed_terms
        d_gram = to_low(d_mix * kern_full)
        dc_mix = jnp.einsum("tsh,sn->tn", d_gram, b_float)
        db_mix = jnp.einsum("tsh,tn->sn", d_gram, c_float)
        ddt_mix = jnp.sum(d_mix * kern_decay * gram_block[:, :, None], axis=0)
        g_scaled = to_low(start_decay[:, :, None] * g_float)
        dc_state = jnp.einsum("thp,hnp->tn", g_scaled, h_low)
        dh_low = jnp.einsum("tn,thp->hnp", c_float, g_scaled)
        d_start = jnp.sum(g_float * from_state, axis=2)
        lam_low = to_low(lam_state)
        d_bw = jnp.einsum("shp,hnp->shn", x_float, lam_low)
        dx_state = jnp.einsum("shn,hnp->shp", b_weighted, lam_low)
        db_state = jnp.sum(d_bw * weight[:, :, None], axis=1)
        d_weight = jnp.sum(d_bw * b_float[:, None, :], axis=2)
        d_decay = jnp.sum(lam_state * h_prev, axis=(1, 2))
        d_total = jnp.sum(d_weight * weight, axis=0) + d_decay * block_decay
        d_cum = jnp.sum(prod_terms, axis=1) - jnp.sum(prod_terms, axis=0) + d_start * start_decay - d_weight * weight
        d_cum = d_cum.at[-1].add(d_total)
        d_log = jnp.cumsum(d_cum[::-1], axis=0)[::-1]
        d_dt = ddt_mix + d_weight * end_decay - decay_rate[None, :] * d_log
        raw_grad = (d_dt * jax.nn.sigmoid(raw_blk.astype(jnp.float32))).astype(jnp.bfloat16)
        rate_grad = -jnp.sum(dt_val * d_log, axis=0) * decay_rate
        dx_total = (d_skip[None, :, None] * g_float + dx_mix + dx_state).astype(jnp.bfloat16)
        new_lam = block_decay[:, None, None] * lam_state + dh_low
        return new_lam, (dx_total, raw_grad, db_mix + db_state, dc_mix + dc_state, rate_grad, skip_grad)

    _, back_outs = lax.scan(backward_step, zero_state,
                            (x_blocks, g_blocks, b_blocks, c_blocks, raw_blocks, seg_blocks, seg_prior, h_all), reverse=True)
    dx_all, raw_all, db_all, dc_all, rate_all, skip_all = back_outs
    mixer_out = y_all.reshape(TOKENS, HEADS * HEAD_DIM)
    grad_inputs = dx_all.reshape(TOKENS, HEADS * HEAD_DIM)
    grad_dt_raw = raw_all.reshape(TOKENS, HEADS)
    grad_b = db_all.reshape(TOKENS, STATE)
    grad_c = dc_all.reshape(TOKENS, STATE)
    grad_a_log = jnp.sum(rate_all, axis=0)
    grad_d_skip = jnp.sum(skip_all, axis=0)
    return (mixer_out, grad_inputs, grad_dt_raw, grad_b, grad_c, grad_a_log, grad_d_skip)
```

```python
import jax
import jax.numpy as jnp
from jax import lax
from jax.experimental import pallas as pl
from jax.experimental.pallas import tpu as pltpu
from jax.sharding import PartitionSpec as P

HEADS = 64
DIM = 64
STATE = 128
BLOCK = 256
WIDTH = HEADS * DIM
CHUNK = 512
STEPS = WIDTH // CHUNK
STEP_HEADS = CHUNK // DIM
TILES = CHUNK // 128
PARTS = 128
PIECE = STATE * WIDTH // (PARTS * 128)
ROWS = STATE // PIECE
META = 16
PAYLOAD = 2 * PIECE + META
LOG2E = 1.4426950408889634
F32 = jnp.float32
BF16 = jnp.bfloat16
VMEM_BYTES = 48 * 1024 * 1024


def dot(a, b):
    return jnp.dot(a, b, preferred_element_type=F32)


def dot_nt(a, b):
    return lax.dot_general(a, b, (((1,), (1,)), ((), ())), preferred_element_type=F32)


def dot_tn(a, b):
    return lax.dot_general(a, b, (((0,), (0,)), ((), ())), preferred_element_type=F32)


def iota(shape, axis):
    return lax.broadcasted_iota(jnp.int32, shape, axis)


def ones_where(mask):
    return jnp.where(mask, 1.0, 0.0).astype(BF16)


def split2(value):
    high = value.astype(BF16)
    return high, (value - high.astype(F32)).astype(BF16)


def split3(value):
    high = value.astype(BF16)
    rest = value - high.astype(F32)
    return (high,) + split2(rest)


def halves(value):
    return jnp.concatenate(split2(value), axis=1)


def dot_exact(ones, value):
    high, mid, low = split3(value)
    return dot(ones, high) + dot(ones, mid) + dot(ones, low)


def spread(head0, lanes):
    shape = (2 * HEADS, lanes)
    return ones_where((iota(shape, 0) & (HEADS - 1)) == (iota(shape, 1) >> 6) + head0)


def gather_heads(head0):
    shape = (256, HEADS)
    return ones_where(((iota(shape, 0) & 127) >> 6) + head0 == iota(shape, 1))


def states_kernel(
    raw_ref, alog_ref, seg_ref, x_ref, g_ref, b_ref, c_ref,
    pay_ref, scal_ref, cumb_ref, cumt_ref, half_ref,
    bt_ref, ct_ref, meta_ref,
):
    step = pl.program_id(0)

    @pl.when(step == 0)
    def _():
        raw = raw_ref[...].astype(F32)
        dt = jnp.maximum(raw, 0.0) + jnp.log1p(jnp.exp(-jnp.abs(raw)))
        rate = jnp.exp(alog_ref[...])
        square = (BLOCK, BLOCK)
        cum = dot_exact(ones_where(iota(square, 0) >= iota(square, 1)), -rate * dt)
        tot = cum[BLOCK - 1 :, :]
        seg_row = seg_ref[...]
        first, last = seg_row[:, :1], seg_row[:, BLOCK - 1 :]
        seg_col = jnp.broadcast_to(seg_row, (128, BLOCK)).T[:, :HEADS]
        end = jnp.where(seg_col == last, jnp.exp(tot - cum), 0.0)
        start = jnp.where(seg_col == first, jnp.exp(cum), 0.0)
        weight = end * dt
        scal_ref[0] = dt
        scal_ref[1] = end
        scal_ref[2] = weight
        scal_ref[3] = start
        cum2 = cum * LOG2E
        for k in range(STEPS):
            cumb_ref[k] = cum2[:, k * STEP_HEADS : (k + 1) * STEP_HEADS]
        cumt_ref[...] = cum2.T
        half_ref[0] = halves(dt)
        half_ref[1] = halves(weight)
        half_ref[2] = halves(start)
        bt_ref[...] = b_ref[...].T
        ct_ref[...] = c_ref[...].T
        high, mid, low = split3(tot)
        kind = iota((META, HEADS), 0)
        rows = jnp.zeros((META, HEADS), F32)
        for k, row in enumerate((high.astype(F32), mid.astype(F32), low.astype(F32), first, last)):
            rows = jnp.where(kind == k, row, rows)
        meta_ref[...] = jnp.concatenate(
            [rows.astype(BF16), jnp.zeros((META, HEADS), BF16)], axis=1
        )

    copy = spread(step * STEP_HEADS, CHUNK)
    meta = dot(meta_ref[...], copy).astype(BF16)
    x_weighted = (x_ref[...].astype(F32) * dot(half_ref[1], copy)).astype(BF16)
    contrib = dot(bt_ref[...], x_weighted).astype(BF16)
    g_scaled = (g_ref[...].astype(F32) * dot(half_ref[2], copy)).astype(BF16)
    dh_low = dot(ct_ref[...], g_scaled).astype(BF16)
    for j in range(TILES):
        lanes = slice(j * 128, (j + 1) * 128)
        for r in range(ROWS):
            rows = slice(r * PIECE, (r + 1) * PIECE)
            pay_ref[j * ROWS + r, :PIECE, :] = contrib[rows, lanes]
            pay_ref[j * ROWS + r, PIECE : 2 * PIECE, :] = dh_low[rows, lanes]
            pay_ref[j * ROWS + r, 2 * PIECE :, :] = meta[:, lanes]


def states(raw, alog, seg, x, g, b, c):
    whole = lambda *shape: pl.BlockSpec(shape, lambda i: (0,) * len(shape))
    wide = pl.BlockSpec((BLOCK, CHUNK), lambda i: (0, i))
    return pl.pallas_call(
        states_kernel,
        grid=(STEPS,),
        in_specs=[
            whole(BLOCK, HEADS), whole(1, HEADS), whole(1, BLOCK), wide, wide,
            whole(BLOCK, STATE), whole(BLOCK, STATE),
        ],
        out_specs=[
            pl.BlockSpec((PARTS // STEPS, PAYLOAD, 128), lambda i: (i, 0, 0)),
            whole(4, BLOCK, HEADS), whole(STEPS, BLOCK, STEP_HEADS), whole(HEADS, BLOCK),
            whole(3, BLOCK, 2 * HEADS),
        ],
        out_shape=[
            jax.ShapeDtypeStruct((PARTS, PAYLOAD, 128), BF16),
            jax.ShapeDtypeStruct((4, BLOCK, HEADS), F32),
            jax.ShapeDtypeStruct((STEPS, BLOCK, STEP_HEADS), F32),
            jax.ShapeDtypeStruct((HEADS, BLOCK), F32),
            jax.ShapeDtypeStruct((3, BLOCK, 2 * HEADS), BF16),
        ],
        scratch_shapes=[
            pltpu.VMEM((STATE, BLOCK), BF16),
            pltpu.VMEM((STATE, BLOCK), BF16),
            pltpu.VMEM((META, 2 * HEADS), BF16),
        ],
        compiler_params=pltpu.CompilerParams(vmem_limit_bytes=VMEM_BYTES),
        cost_estimate=pl.CostEstimate(flops=10**9, bytes_accessed=8 * 10**6, transcendentals=10**5),
        name="states",
    )(raw, alog, seg, x, g, b, c)


def mix_kernel(
    x_ref, g_ref, b_ref, c_ref, seg_ref, skip_ref, cumb_ref, cumt_ref, half_ref,
    y_ref, dx_ref, cpart_ref, ddt_ref, db_ref, dc_ref, dskip_ref,
    gram_ref, mask_ref, total_ref,
):
    step = pl.program_id(0)
    square = (BLOCK, BLOCK)

    @pl.when(step == 0)
    def _():
        seg_row = seg_ref[...]
        seg_col = jnp.broadcast_to(seg_row, square).T
        keep = (seg_row == seg_col) & (iota(square, 0) >= iota(square, 1))
        mask_ref[...] = jnp.where(keep, 0.0, -1e30)
        gram_ref[...] = dot_nt(c_ref[...], b_ref[...])
        total_ref[...] = jnp.zeros_like(total_ref)
        cpart_ref[...] = jnp.zeros_like(cpart_ref)
        ddt_ref[...] = jnp.zeros_like(ddt_ref)
        dskip_ref[...] = jnp.zeros_like(dskip_ref)

    lower = iota((BLOCK, 128), 1) < DIM
    zero = jnp.zeros((BLOCK, 128), BF16)
    for j in range(TILES):
        head0 = step * STEP_HEADS + 2 * j
        lanes = slice(j * 128, (j + 1) * 128)
        x_low = x_ref[:, lanes]
        g_low = g_ref[:, lanes]
        x = x_low.astype(F32)
        g = g_low.astype(F32)
        dt = dot(half_ref[0], spread(head0, 128))
        x_dt = (x * dt).astype(BF16)
        y = jnp.zeros((BLOCK, 128), F32)
        dx = jnp.zeros((BLOCK, 128), F32)
        for k in range(2):
            pick = lower if k == 0 else ~lower
            g_one = jnp.where(pick, g_low, zero)
            x_one = jnp.where(pick, x_dt, zero)
            col = cumb_ref[0, :, 2 * j + k : 2 * j + k + 1]
            row = cumt_ref[2 * j + k : 2 * j + k + 1, :]
            kern = jnp.exp2(col - row + mask_ref[...])
            mixed = (gram_ref[...] * kern).astype(BF16)
            total_ref[...] += dot_nt(g_one, x_dt) * kern
            y += dot(mixed, x_one)
            dx += dot_tn(mixed, g_one)
        skip = skip_ref[:, lanes]
        gather = gather_heads(head0)
        y_ref[:, lanes] = (y + skip * x).astype(BF16)
        dx_ref[:, lanes] = (dx * dt + skip * g).astype(BF16)
        cpart_ref[...] += dot(halves(g * y - x_dt.astype(F32) * dx), gather)
        ddt_ref[...] += dot(halves(x * dx), gather)
        channel_sum = jnp.broadcast_to(jnp.sum(g * x, axis=0, keepdims=True), (8, 128))
        dskip_ref[...] += dot(halves(channel_sum), gather)

    @pl.when(step == STEPS - 1)
    def _():
        total = total_ref[...].astype(BF16)
        dc_ref[...] = dot(total, b_ref[...])
        db_ref[...] = dot_tn(total, c_ref[...])


def mix(x, g, b, c, seg, skip, cumb, cumt, half):
    whole = lambda *shape: pl.BlockSpec(shape, lambda i: (0,) * len(shape))
    wide = pl.BlockSpec((BLOCK, CHUNK), lambda i: (0, i))
    return pl.pallas_call(
        mix_kernel,
        grid=(STEPS,),
        in_specs=[
            wide, wide, whole(BLOCK, STATE), whole(BLOCK, STATE), whole(1, BLOCK),
            pl.BlockSpec((1, CHUNK), lambda i: (0, i)),
            pl.BlockSpec((1, BLOCK, STEP_HEADS), lambda i: (i, 0, 0)),
            pl.BlockSpec((STEP_HEADS, BLOCK), lambda i: (i, 0)),
            whole(3, BLOCK, 2 * HEADS),
        ],
        out_specs=[
            wide, wide, whole(BLOCK, HEADS), whole(BLOCK, HEADS),
            whole(BLOCK, STATE), whole(BLOCK, STATE), whole(8, HEADS),
        ],
        out_shape=[
            jax.ShapeDtypeStruct((BLOCK, WIDTH), BF16),
            jax.ShapeDtypeStruct((BLOCK, WIDTH), BF16),
            jax.ShapeDtypeStruct((BLOCK, HEADS), F32),
            jax.ShapeDtypeStruct((BLOCK, HEADS), F32),
            jax.ShapeDtypeStruct((BLOCK, STATE), F32),
            jax.ShapeDtypeStruct((BLOCK, STATE), F32),
            jax.ShapeDtypeStruct((8, HEADS), F32),
        ],
        scratch_shapes=[
            pltpu.VMEM((BLOCK, BLOCK), F32),
            pltpu.VMEM((BLOCK, BLOCK), F32),
            pltpu.VMEM((BLOCK, BLOCK), F32),
        ],
        compiler_params=pltpu.CompilerParams(vmem_limit_bytes=VMEM_BYTES),
        cost_estimate=pl.CostEstimate(
            flops=20 * 10**9, bytes_accessed=9 * 10**6, transcendentals=4 * 10**6
        ),
        name="mix",
    )(x, g, b, c, seg, skip, cumb, cumt, half)


def scan_kernel(pay_ref, out_ref, wide_ref, done_ref):
    wide_ref[...] = pay_ref[...].reshape(PARTS * PAYLOAD, 128).astype(F32)

    def row_of(k):
        return wide_ref[pl.ds(k, PARTS, stride=PAYLOAD), :]

    square = (PARTS, PARTS)
    high, mid, low, first, last = (row_of(2 * PIECE + k) for k in range(5))
    parts = (high.astype(BF16), mid.astype(BF16), low.astype(BF16))
    upto = ones_where(iota(square, 0) >= iota(square, 1))
    before = ones_where(iota(square, 0) > iota(square, 1))
    through = dot(upto, parts[0]) + dot(upto, parts[1]) + dot(upto, parts[2])
    ahead = dot(before, parts[0]) + dot(before, parts[1]) + dot(before, parts[2])
    through_t = through.T
    last_t = last.T
    earlier = iota(square, 0) > iota(square, 1)
    carries = []
    for lane in (0, DIM):
        gap = ahead[:, lane : lane + 1] - through_t[lane : lane + 1, :]
        keep = earlier & (first[:, lane : lane + 1] == last_t[lane : lane + 1, :])
        carries.append(jnp.where(keep, jnp.exp(jnp.minimum(gap, 0.0)), 0.0))
    forward = jnp.concatenate(carries, axis=1).astype(BF16)
    backward = jnp.concatenate([carry.T for carry in carries], axis=1).astype(BF16)
    lower = iota((PARTS, 128), 1) < DIM

    def both(k):
        row = row_of(k)
        return jnp.concatenate(
            [jnp.where(lower, row, 0.0), jnp.where(lower, 0.0, row)], axis=0
        ).astype(BF16)

    for k in range(0, 2 * PIECE, 2):
        carry = forward if k < PIECE else backward
        pair = dot(carry, jnp.concatenate([both(k), both(k + 1)], axis=1))
        done_ref[pl.ds(k, PARTS, stride=2 * PIECE), :] = pair[:, :128]
        done_ref[pl.ds(k + 1, PARTS, stride=2 * PIECE), :] = pair[:, 128:]
    out_ref[...] = done_ref[...].astype(BF16).reshape(PARTS, 2 * PIECE, 128)


def scan(pay):
    return pl.pallas_call(
        scan_kernel,
        out_shape=jax.ShapeDtypeStruct((PARTS, 2 * PIECE, 128), BF16),
        in_specs=[pl.BlockSpec(memory_space=pltpu.VMEM)],
        out_specs=pl.BlockSpec(memory_space=pltpu.VMEM),
        scratch_shapes=[
            pltpu.VMEM((PARTS * PAYLOAD, 128), F32),
            pltpu.VMEM((PARTS * 2 * PIECE, 128), F32),
        ],
        compiler_params=pltpu.CompilerParams(vmem_limit_bytes=VMEM_BYTES),
        cost_estimate=pl.CostEstimate(
            flops=5 * 10**8, bytes_accessed=5 * 10**6, transcendentals=10**5
        ),
        name="scan",
    )(pay)


def finish_kernel(
    x_ref, g_ref, ymix_ref, dxmix_ref, state_ref, b_ref, c_ref, half_ref, scal_ref,
    raw_ref, alog_ref, seg_ref, cpart_ref, ddt_ref, dbmix_ref, dcmix_ref, dskip_ref,
    y_ref, dx_ref, raw_grad_ref, db_ref, dc_ref, sums_ref,
    dstart_ref, dweight_ref, ddecay_ref,
):
    step = pl.program_id(0)

    @pl.when(step == 0)
    def _():
        db_ref[...] = dbmix_ref[...]
        dc_ref[...] = dcmix_ref[...]
        dstart_ref[...] = jnp.zeros_like(dstart_ref)
        dweight_ref[...] = jnp.zeros_like(dweight_ref)
        ddecay_ref[...] = jnp.zeros_like(ddecay_ref)

    for j in range(TILES):
        head0 = step * STEP_HEADS + 2 * j
        lanes = slice(j * 128, (j + 1) * 128)
        copy = spread(head0, 128)
        gather = gather_heads(head0)
        x = x_ref[:, lanes].astype(F32)
        g = g_ref[:, lanes].astype(F32)
        tile = state_ref[j * ROWS : (j + 1) * ROWS]
        h_low = tile[:, :PIECE].reshape(STATE, 128)
        lam_low = tile[:, PIECE:].reshape(STATE, 128)
        start = dot(half_ref[2], copy)
        weight = dot(half_ref[1], copy)
        from_state = dot(c_ref[...], h_low)
        from_grad = dot(b_ref[...], lam_low)
        y_ref[:, lanes] = (ymix_ref[:, lanes].astype(F32) + start * from_state).astype(BF16)
        dx_ref[:, lanes] = (dxmix_ref[:, lanes].astype(F32) + weight * from_grad).astype(BF16)
        dc_ref[...] += dot_nt((start * g).astype(BF16), h_low)
        db_ref[...] += dot_nt((weight * x).astype(BF16), lam_low)
        dstart_ref[...] += dot(halves(g * from_state), gather)
        dweight_ref[...] += dot(halves(x * from_grad), gather)
        channel_sum = jnp.sum(h_low.astype(F32) * lam_low.astype(F32), axis=0, keepdims=True)
        ddecay_ref[...] += dot(halves(jnp.broadcast_to(channel_sum, (8, 128))), gather)

    @pl.when(step == STEPS - 1)
    def _():
        dt, end, weight, start = (scal_ref[k] for k in range(4))
        d_weight = dweight_ref[...]
        used = d_weight * weight
        d_cum = cpart_ref[...] + dstart_ref[...] * start - used
        at_last = iota((BLOCK, HEADS), 0) == BLOCK - 1
        d_total = jnp.sum(used, axis=0, keepdims=True) + ddecay_ref[:1] * start[BLOCK - 1 :]
        d_cum = d_cum + jnp.where(at_last, d_total, 0.0)
        square = (BLOCK, BLOCK)
        d_log = dot_exact(ones_where(iota(square, 0) <= iota(square, 1)), d_cum)
        rate = jnp.exp(alog_ref[...])
        d_dt = ddt_ref[...] + d_weight * end - rate * d_log
        raw = raw_ref[...].astype(F32)
        raw_grad_ref[...] = (d_dt / (1.0 + jnp.exp(-raw))).astype(BF16)
        rate_grad = -jnp.sum(dt * d_log, axis=0, keepdims=True) * rate
        sums = jnp.concatenate([rate_grad, dskip_ref[:1]], axis=1)
        sums_ref[...] = jnp.broadcast_to(sums, (PARTS, 128))


def finish(x, g, ymix, dxmix, state, b, c, half, scal, raw, alog, seg, cpart, ddt, dbmix, dcmix, dskip):
    whole = lambda *shape: pl.BlockSpec(shape, lambda i: (0,) * len(shape))
    wide = pl.BlockSpec((BLOCK, CHUNK), lambda i: (0, i))
    return pl.pallas_call(
        finish_kernel,
        grid=(STEPS,),
        in_specs=[
            wide, wide, wide, wide,
            pl.BlockSpec((PARTS // STEPS, 2 * PIECE, 128), lambda i: (i, 0, 0)),
            whole(BLOCK, STATE), whole(BLOCK, STATE), whole(3, BLOCK, 2 * HEADS),
            whole(4, BLOCK, HEADS), whole(BLOCK, HEADS), whole(1, HEADS), whole(1, BLOCK),
            whole(BLOCK, HEADS), whole(BLOCK, HEADS),
            whole(BLOCK, STATE), whole(BLOCK, STATE), whole(8, HEADS),
        ],
        out_specs=[
            wide, wide, whole(BLOCK, HEADS), whole(BLOCK, STATE), whole(BLOCK, STATE),
            whole(PARTS, 128),
        ],
        out_shape=[
            jax.ShapeDtypeStruct((BLOCK, WIDTH), BF16),
            jax.ShapeDtypeStruct((BLOCK, WIDTH), BF16),
            jax.ShapeDtypeStruct((BLOCK, HEADS), BF16),
            jax.ShapeDtypeStruct((BLOCK, STATE), F32),
            jax.ShapeDtypeStruct((BLOCK, STATE), F32),
            jax.ShapeDtypeStruct((PARTS, 128), F32),
        ],
        scratch_shapes=[
            pltpu.VMEM((BLOCK, HEADS), F32),
            pltpu.VMEM((BLOCK, HEADS), F32),
            pltpu.VMEM((8, HEADS), F32),
        ],
        compiler_params=pltpu.CompilerParams(vmem_limit_bytes=VMEM_BYTES),
        cost_estimate=pl.CostEstimate(
            flops=2 * 10**9, bytes_accessed=16 * 10**6, transcendentals=10**5
        ),
        name="finish",
    )(x, g, ymix, dxmix, state, b, c, half, scal, raw, alog, seg, cpart, ddt, dbmix, dcmix, dskip)


def body(inputs, dt_raw, b_proj, c_proj, a_log, d_skip, seg_ids, cotangent):
    everyone = ("seq", "head")
    mine = lax.axis_index("head")
    group = a_log.shape[0]
    gains = lax.all_gather(jnp.stack([a_log, d_skip]), "head")
    alog = gains[:, 0].reshape(1, HEADS)
    skip = jnp.broadcast_to(gains[:, 1].reshape(HEADS, 1), (HEADS, DIM)).reshape(1, WIDTH)
    seg = lax.dynamic_slice(seg_ids, (mine * BLOCK,), (BLOCK,)).astype(F32).reshape(1, BLOCK)
    pay, scal, cumb, cumt, half = states(dt_raw, alog, seg, inputs, cotangent, b_proj, c_proj)
    pay = lax.all_to_all(pay, everyone, 0, 0, tiled=True)
    ymix, dxmix, cpart, ddt, dbmix, dcmix, dskip = mix(
        inputs, cotangent, b_proj, c_proj, seg, skip, cumb, cumt, half
    )
    state = lax.all_to_all(scan(pay), everyone, 0, 0, tiled=True)
    y, dx, raw_grad, db, dc, sums = finish(
        inputs, cotangent, ymix, dxmix, state, b_proj, c_proj, half, scal, dt_raw, alog, seg,
        cpart, ddt, dbmix, dcmix, dskip,
    )
    sums = lax.all_to_all(sums.reshape(PARTS, 1, 128), everyone, 0, 0, tiled=True)
    sums = jnp.sum(sums, axis=(0, 1))
    a_grad = lax.dynamic_slice(sums, (mine * group,), (group,))
    skip_grad = lax.dynamic_slice(sums, (HEADS + mine * group,), (group,))
    return (y, dx, raw_grad, db, dc, a_grad, skip_grad)


def solution(mesh):
    tokens = P(("seq", "head"), None)
    in_specs = (tokens, tokens, tokens, tokens, P("head"), P("head"), P("seq"), tokens)
    out_specs = (tokens, tokens, tokens, tokens, tokens, P("head"), P("head"))
    return jax.shard_map(body, mesh=mesh, in_specs=in_specs, out_specs=out_specs, check_vma=False)
```

```python
import jax
import jax.numpy as jnp
from jax import lax
from jax.experimental import pallas as pl
from jax.experimental.pallas import tpu as pltpu
from jax.sharding import PartitionSpec as P

HEADS = 64
DIM = 64
STATE = 128
BLOCK = 256
WIDTH = HEADS * DIM
PARTS = 128
PIECE = STATE * WIDTH // (PARTS * 128)
ROWS = STATE // PIECE
CARRY = 2 * PIECE
META = 8
LOG2E = 1.4426950408889634
F32 = jnp.float32
BF16 = jnp.bfloat16


def dot(a, b):
    return jnp.dot(a, b, preferred_element_type=F32)


def dot_nt(a, b):
    return lax.dot_general(a, b, (((1,), (1,)), ((), ())), preferred_element_type=F32)


def dot_tn(a, b):
    return lax.dot_general(a, b, (((0,), (0,)), ((), ())), preferred_element_type=F32)


def iota(shape, axis):
    return lax.broadcasted_iota(jnp.int32, shape, axis)


def ones_where(mask):
    return jnp.where(mask, 1.0, 0.0).astype(BF16)


def split2(value):
    high = value.astype(BF16)
    return high, (value - high.astype(F32)).astype(BF16)


def split3(value):
    high = value.astype(BF16)
    return (high,) + split2(value - high.astype(F32))


def spread(head0, lanes):
    shape = (2 * HEADS, lanes)
    return ones_where((iota(shape, 0) & (HEADS - 1)) == (iota(shape, 1) >> 6) + head0)


def gather_heads(head0, lanes, period):
    shape = (lanes, HEADS)
    return ones_where(((iota(shape, 0) & (period - 1)) >> 6) + head0 == iota(shape, 1))


def whole(*shape):
    return pl.BlockSpec(shape, lambda *_: (0,) * len(shape))


def wide(lanes):
    return pl.BlockSpec((BLOCK, lanes), lambda i: (0, i))


def pieces(lanes, rows):
    return pl.BlockSpec((PARTS * lanes // WIDTH, rows, 128), lambda i: (i, 0, 0))


def params(mib=24):
    return pltpu.CompilerParams(vmem_limit_bytes=mib * 1024 * 1024)


def cost(flops, moved, exps):
    return pl.CostEstimate(flops=flops, bytes_accessed=moved, transcendentals=exps)


def like(shape, kind=F32):
    return jax.ShapeDtypeStruct(shape, kind)


STATES_LANES = 1024


def states_kernel(
    place_ref, raw_ref, gains_ref, seg_ref, x_ref, g_ref, b_ref, c_ref,
    pay_ref, scal_ref, cum2_ref, half_ref, rate_ref, row_ref,
    bt_ref, ct_ref, meta_ref,
):
    step = pl.program_id(0)

    @pl.when(step == 0)
    def _():
        raw = raw_ref[...].astype(F32)
        dt = jnp.maximum(raw, 0.0) + jnp.log1p(jnp.exp(-jnp.abs(raw)))
        square = (BLOCK, BLOCK)
        upto = ones_where(iota(square, 0) <= iota(square, 1))
        high, mid, low = split3(dt)
        sums = dot(high, upto) + dot(mid, upto) + dot(low, upto)
        gains = gains_ref[...]
        alog = jnp.concatenate([gains[k : k + 1] for k in range(0, gains.shape[0], 2)], axis=1)
        rate = jnp.exp(jnp.broadcast_to(alog, (128, HEADS)).T)
        cum = -rate[:, :1] * sums
        tot = cum[:, BLOCK - 1 :]
        block = 2 * (place_ref[0] % (seg_ref.shape[0] // 2))
        seg = jnp.concatenate(
            [seg_ref[pl.ds(block, 1), :], seg_ref[pl.ds(block + 1, 1), :]], axis=1
        ).astype(F32)
        first, last = seg[:, :1], seg[:, BLOCK - 1 :]
        end = jnp.where(seg == last, jnp.exp(tot - cum), 0.0)
        start = jnp.where(seg == first, jnp.exp(cum), 0.0)
        weight = end * dt
        scal_ref[0] = end
        scal_ref[1] = weight
        scal_ref[2] = start
        scal_ref[3] = dt
        cum2_ref[...] = cum * LOG2E
        half_ref[0] = jnp.concatenate(split2(weight), axis=0).T
        half_ref[1] = jnp.concatenate(split2(start), axis=0).T
        half_ref[2] = jnp.concatenate(split2(dt), axis=0).T
        rate_ref[...] = rate
        row_ref[...] = seg
        bt_ref[...] = b_ref[...].T
        ct_ref[...] = c_ref[...].T
        kind = iota((HEADS, 128), 1)
        columns = jnp.zeros((HEADS, 128), F32)
        for k, part in enumerate(split3(tot)):
            columns = jnp.where(kind == k, part.astype(F32), columns)
        columns = jnp.where(kind == 3, first, jnp.where(kind == 4, last, columns))
        rows = jnp.concatenate([columns, jnp.zeros((HEADS, 128), F32)], axis=0).T
        meta_ref[...] = rows[:16].astype(BF16)

    copy = spread(step * (STATES_LANES // DIM), STATES_LANES)
    meta = dot(meta_ref[...], copy)[:META].astype(BF16)
    x_weighted = (x_ref[...].astype(F32) * dot(half_ref[0], copy)).astype(BF16)
    contrib = dot(bt_ref[...], x_weighted).astype(BF16)
    g_scaled = (g_ref[...].astype(F32) * dot(half_ref[1], copy)).astype(BF16)
    dh_low = dot(ct_ref[...], g_scaled).astype(BF16)
    for j in range(STATES_LANES // 128):
        lanes = slice(j * 128, (j + 1) * 128)
        for r in range(ROWS):
            rows = slice(r * PIECE, (r + 1) * PIECE)
            pay_ref[j * ROWS + r, :PIECE, :] = contrib[rows, lanes]
            pay_ref[j * ROWS + r, PIECE:CARRY, :] = dh_low[rows, lanes]
            pay_ref[j * ROWS + r, CARRY:, :] = meta[:, lanes]


def states(place, raw_t, gains, seg_ids, x, g, b, c):
    return pl.pallas_call(
        states_kernel,
        grid=(WIDTH // STATES_LANES,),
        in_specs=[
            pl.BlockSpec(memory_space=pltpu.SMEM),
            whole(HEADS, BLOCK), whole(*gains.shape), whole(*seg_ids.shape),
            wide(STATES_LANES), wide(STATES_LANES), whole(BLOCK, STATE), whole(BLOCK, STATE),
        ],
        out_specs=[
            pieces(STATES_LANES, CARRY + META), whole(4, HEADS, BLOCK), whole(HEADS, BLOCK),
            whole(3, BLOCK, 2 * HEADS), whole(HEADS, 128), whole(1, BLOCK),
        ],
        out_shape=[
            like((PARTS, CARRY + META, 128), BF16), like((4, HEADS, BLOCK)), like((HEADS, BLOCK)),
            like((3, BLOCK, 2 * HEADS), BF16), like((HEADS, 128)), like((1, BLOCK)),
        ],
        scratch_shapes=[
            pltpu.VMEM((STATE, BLOCK), BF16),
            pltpu.VMEM((STATE, BLOCK), BF16),
            pltpu.VMEM((16, 2 * HEADS), BF16),
        ],
        compiler_params=params(),
        cost_estimate=cost(10**9, 8 * 10**6, 10**5),
        name="states",
    )(place, raw_t, gains, seg_ids, x, g, b, c)


MIX_LANES = 512


def mix_kernel(
    x_ref, g_ref, b_ref, c_ref, seg_ref, skip_ref, cum2_ref, half_ref,
    y_ref, dx_ref, cpart_ref, ddt_ref, db_ref, dc_ref, dskip_ref,
    gram_ref, mask_ref, total_ref, cpart_sum_ref, ddt_sum_ref, dskip_sum_ref,
):
    step = pl.program_id(0)
    square = (BLOCK, BLOCK)

    @pl.when(step == 0)
    def _():
        seg_row = seg_ref[...]
        seg_col = jnp.broadcast_to(seg_row, square).T
        keep = (seg_row == seg_col) & (iota(square, 0) >= iota(square, 1))
        mask_ref[...] = jnp.where(keep, 0.0, -1e30)
        gram_ref[...] = dot_nt(c_ref[...], b_ref[...])
        total_ref[...] = jnp.zeros_like(total_ref)
        cpart_sum_ref[...] = jnp.zeros_like(cpart_sum_ref)
        ddt_sum_ref[...] = jnp.zeros_like(ddt_sum_ref)
        dskip_sum_ref[...] = jnp.zeros_like(dskip_sum_ref)

    lower = iota((BLOCK, 128), 1) < DIM
    zero = jnp.zeros((BLOCK, 128), BF16)
    cum2 = cum2_ref[...]
    columns = cum2.T
    for j in range(MIX_LANES // 128):
        head0 = step * (MIX_LANES // DIM) + 2 * j
        lanes = slice(j * 128, (j + 1) * 128)
        x_low = x_ref[:, lanes]
        g_low = g_ref[:, lanes]
        x = x_low.astype(F32)
        g = g_low.astype(F32)
        dt = dot(half_ref[2], spread(head0, 128))
        x_dt = (x * dt).astype(BF16)
        y = jnp.zeros((BLOCK, 128), F32)
        dx = jnp.zeros((BLOCK, 128), F32)
        for k in range(2):
            pick = lower if k == 0 else ~lower
            g_one = jnp.where(pick, g_low, zero)
            x_one = jnp.where(pick, x_dt, zero)
            head = 2 * j + k
            gap = columns[:, head : head + 1] - cum2[head : head + 1, :]
            kern = jnp.exp2(gap + mask_ref[...])
            mixed = (gram_ref[...] * kern).astype(BF16)
            total_ref[...] += dot_nt(g_one, x_dt) * kern
            y += dot(mixed, x_one)
            dx += dot_tn(mixed, g_one)
        skip = skip_ref[:, lanes]
        gather = gather_heads(head0, 256, 128)
        y_ref[:, lanes] = (y + skip * x).astype(BF16)
        dx_ref[:, lanes] = (dx * dt + skip * g).astype(BF16)
        apart = jnp.concatenate(split2(g * y - x_dt.astype(F32) * dx), axis=1)
        cpart_sum_ref[...] += dot(apart, gather)
        ddt_sum_ref[...] += dot((x * dx).astype(BF16), gather[:128])
        channel_sum = jnp.broadcast_to(jnp.sum(g * x, axis=0, keepdims=True), (8, 128))
        dskip_sum_ref[...] += dot(jnp.concatenate(split2(channel_sum), axis=1), gather)

    @pl.when(step == WIDTH // MIX_LANES - 1)
    def _():
        total = total_ref[...].astype(BF16)
        dc_ref[...] = dot(total, b_ref[...])
        db_ref[...] = dot_tn(total, c_ref[...])
        cpart_ref[...] = cpart_sum_ref[...].T
        ddt_ref[...] = ddt_sum_ref[...].T
        dskip_ref[...] = jnp.broadcast_to(dskip_sum_ref[:1], (128, HEADS)).T


def mix(x, g, b, c, seg, skip, cum2, half):
    return pl.pallas_call(
        mix_kernel,
        grid=(WIDTH // MIX_LANES,),
        in_specs=[
            wide(MIX_LANES), wide(MIX_LANES), whole(BLOCK, STATE), whole(BLOCK, STATE),
            whole(1, BLOCK),
            pl.BlockSpec((1, MIX_LANES), lambda i: (0, i)),
            pl.BlockSpec((MIX_LANES // DIM, BLOCK), lambda i: (i, 0)),
            whole(3, BLOCK, 2 * HEADS),
        ],
        out_specs=[
            wide(MIX_LANES), wide(MIX_LANES), whole(HEADS, BLOCK), whole(HEADS, BLOCK),
            whole(BLOCK, STATE), whole(BLOCK, STATE), whole(HEADS, 128),
        ],
        out_shape=[
            like((BLOCK, WIDTH), BF16), like((BLOCK, WIDTH), BF16),
            like((HEADS, BLOCK)), like((HEADS, BLOCK)),
            like((BLOCK, STATE)), like((BLOCK, STATE)), like((HEADS, 128)),
        ],
        scratch_shapes=[pltpu.VMEM((BLOCK, BLOCK), F32)] * 3
        + [pltpu.VMEM((BLOCK, HEADS), F32)] * 2
        + [pltpu.VMEM((8, HEADS), F32)],
        compiler_params=params(),
        cost_estimate=cost(20 * 10**9, 9 * 10**6, 4 * 10**6),
        name="mix",
    )(x, g, b, c, seg, skip, cum2, half)


def scan_kernel(pay_ref, out_ref, wide_ref, done_ref):
    wide_ref[...] = pay_ref[...].astype(F32)

    def row_of(k):
        return wide_ref[:, k, :]

    square = (PARTS, PARTS)
    high, mid, low, first, last = (row_of(CARRY + k) for k in range(5))
    upto = ones_where(iota(square, 0) >= iota(square, 1))
    through = dot(upto, high.astype(BF16)) + dot(upto, mid.astype(BF16)) + dot(upto, low.astype(BF16))
    ahead = through - (high + mid + low)
    through_t = through.T
    keep = (iota(square, 0) > iota(square, 1)) & (first[:, :1] == last.T[:1, :])
    forward, backward = [], []
    for lane in (0, DIM):
        gap = ahead[:, lane : lane + 1] - through_t[lane : lane + 1, :]
        carry = jnp.where(keep, jnp.exp(jnp.minimum(gap, 0.0)), 0.0)
        forward.append(carry.astype(BF16))
        backward.append(carry.T.astype(BF16))
    forward = jnp.concatenate(forward, axis=0)
    backward = jnp.concatenate(backward, axis=0)
    lower = iota((PARTS, 256), 1) & (128 - 1) < DIM

    for k in range(0, CARRY, 2):
        rows = jnp.concatenate([row_of(k), row_of(k + 1)], axis=1).astype(BF16)
        both = dot(forward if k < PIECE else backward, rows)
        pair = jnp.where(lower, both[:PARTS], both[PARTS:])
        done_ref[:, k, :] = pair[:, :128]
        done_ref[:, k + 1, :] = pair[:, 128:]
    out_ref[...] = done_ref[...].astype(BF16)


def scan(pay):
    return pl.pallas_call(
        scan_kernel,
        out_shape=like((PARTS, CARRY, 128), BF16),
        in_specs=[pl.BlockSpec(memory_space=pltpu.VMEM)],
        out_specs=pl.BlockSpec(memory_space=pltpu.VMEM),
        scratch_shapes=[
            pltpu.VMEM((PARTS, CARRY + META, 128), F32),
            pltpu.VMEM((PARTS, CARRY, 128), F32),
        ],
        compiler_params=params(),
        cost_estimate=cost(5 * 10**8, 5 * 10**6, 10**5),
        name="scan",
    )(pay)


def carried(state_ref, j):
    tiles = [state_ref[k * ROWS : (k + 1) * ROWS] for k in (2 * j, 2 * j + 1)]
    h_low = jnp.concatenate([tile[:, :PIECE].reshape(STATE, 128) for tile in tiles], axis=1)
    lam_low = jnp.concatenate([tile[:, PIECE:].reshape(STATE, 128) for tile in tiles], axis=1)
    return h_low, lam_low


SUMS_LANES = 1024


def sums_kernel(
    x_ref, g_ref, state_ref, b_ref, c_ref, scal_ref, raw_ref, rate_ref,
    cpart_ref, ddt_ref, dskip_ref,
    raw_grad_ref, sums_ref,
    dstart_ref, dweight_ref, ddecay_ref,
):
    step = pl.program_id(0)

    @pl.when(step == 0)
    def _():
        dstart_ref[...] = jnp.zeros_like(dstart_ref)
        dweight_ref[...] = jnp.zeros_like(dweight_ref)
        ddecay_ref[...] = jnp.zeros_like(ddecay_ref)

    for j in range(SUMS_LANES // 256):
        lanes = slice(j * 256, (j + 1) * 256)
        gather = gather_heads(step * (SUMS_LANES // DIM) + 4 * j, 256, 256)
        h_low, lam_low = carried(state_ref, j)
        from_state = dot(c_ref[...], h_low)
        from_grad = dot(b_ref[...], lam_low)
        dstart_ref[...] += dot((g_ref[:, lanes].astype(F32) * from_state).astype(BF16), gather)
        dweight_ref[...] += dot((x_ref[:, lanes].astype(F32) * from_grad).astype(BF16), gather)
        ddecay_ref[...] += dot((h_low.astype(F32) * lam_low.astype(F32)).astype(BF16), gather)

    @pl.when(step == WIDTH // SUMS_LANES - 1)
    def _():
        end, weight, start, dt = (scal_ref[k] for k in range(4))
        d_weight = dweight_ref[...].T
        used = d_weight * weight
        d_cum = cpart_ref[...] + dstart_ref[...].T * start - used
        at_last = iota((HEADS, BLOCK), 1) == BLOCK - 1
        d_decay = jnp.sum(ddecay_ref[...].T, axis=1, keepdims=True)
        d_total = jnp.sum(used, axis=1, keepdims=True) + d_decay * start[:, BLOCK - 1 :]
        d_cum = d_cum + jnp.where(at_last, d_total, 0.0)
        square = (BLOCK, BLOCK)
        onward = ones_where(iota(square, 0) >= iota(square, 1))
        high, mid, low = split3(d_cum)
        d_log = dot(high, onward) + dot(mid, onward) + dot(low, onward)
        rate = rate_ref[:, :1]
        d_dt = ddt_ref[...] + d_weight * end - rate * d_log
        raw = raw_ref[...].astype(F32)
        raw_grad_ref[...] = (d_dt / (1.0 + jnp.exp(-raw))).astype(BF16)
        rate_grad = -jnp.sum(dt * d_log, axis=1, keepdims=True) * rate
        column = jnp.concatenate([rate_grad, dskip_ref[:, :1]], axis=0)
        sums_ref[...] = jnp.broadcast_to(column, (PARTS, 128)).T


def gradient_sums(x, g, state, b, c, scal, raw_t, rate, cpart, ddt, dskip):
    return pl.pallas_call(
        sums_kernel,
        grid=(WIDTH // SUMS_LANES,),
        in_specs=[
            wide(SUMS_LANES), wide(SUMS_LANES), pieces(SUMS_LANES, CARRY),
            whole(BLOCK, STATE), whole(BLOCK, STATE),
            whole(4, HEADS, BLOCK), whole(HEADS, BLOCK), whole(HEADS, 128),
            whole(HEADS, BLOCK), whole(HEADS, BLOCK), whole(HEADS, 128),
        ],
        out_specs=[whole(HEADS, BLOCK), whole(PARTS, 128)],
        out_shape=[like((HEADS, BLOCK), BF16), like((PARTS, 128))],
        scratch_shapes=[
            pltpu.VMEM((BLOCK, HEADS), F32),
            pltpu.VMEM((BLOCK, HEADS), F32),
            pltpu.VMEM((STATE, HEADS), F32),
        ],
        compiler_params=params(),
        cost_estimate=cost(10**9, 8 * 10**6, 10**5),
        name="gradient_sums",
    )(x, g, state, b, c, scal, raw_t, rate, cpart, ddt, dskip)


FINISH_LANES = 512


def finish_kernel(
    x_ref, g_ref, ymix_ref, dxmix_ref, state_ref, b_ref, c_ref, half_ref, dbmix_ref, dcmix_ref,
    y_ref, dx_ref, db_ref, dc_ref,
):
    step = pl.program_id(0)

    @pl.when(step == 0)
    def _():
        db_ref[...] = dbmix_ref[...]
        dc_ref[...] = dcmix_ref[...]

    for j in range(FINISH_LANES // 256):
        copy = spread(step * (FINISH_LANES // DIM) + 4 * j, 256)
        lanes = slice(j * 256, (j + 1) * 256)
        x = x_ref[:, lanes].astype(F32)
        g = g_ref[:, lanes].astype(F32)
        h_low, lam_low = carried(state_ref, j)
        weight = dot(half_ref[0], copy)
        start = dot(half_ref[1], copy)
        from_state = dot(c_ref[...], h_low)
        from_grad = dot(b_ref[...], lam_low)
        y_ref[:, lanes] = (ymix_ref[:, lanes].astype(F32) + start * from_state).astype(BF16)
        dx_ref[:, lanes] = (dxmix_ref[:, lanes].astype(F32) + weight * from_grad).astype(BF16)
        dc_ref[...] += dot_nt((start * g).astype(BF16), h_low)
        db_ref[...] += dot_nt((weight * x).astype(BF16), lam_low)


def finish(x, g, ymix, dxmix, state, b, c, half, dbmix, dcmix):
    lanes = FINISH_LANES
    return pl.pallas_call(
        finish_kernel,
        grid=(WIDTH // lanes,),
        in_specs=[
            wide(lanes), wide(lanes), wide(lanes), wide(lanes), pieces(lanes, CARRY),
            whole(BLOCK, STATE), whole(BLOCK, STATE),
            whole(3, BLOCK, 2 * HEADS), whole(BLOCK, STATE), whole(BLOCK, STATE),
        ],
        out_specs=[wide(lanes), wide(lanes), whole(BLOCK, STATE), whole(BLOCK, STATE)],
        out_shape=[
            like((BLOCK, WIDTH), BF16), like((BLOCK, WIDTH), BF16),
            like((BLOCK, STATE)), like((BLOCK, STATE)),
        ],
        compiler_params=params(),
        cost_estimate=cost(8 * 10**9, 16 * 10**6, 10**5),
        name="finish",
    )(x, g, ymix, dxmix, state, b, c, half, dbmix, dcmix)


def body(inputs, dt_raw, b_proj, c_proj, a_log, d_skip, seg_ids, cotangent):
    everyone = ("seq", "head")
    mine = lax.axis_index("head")
    place = mine.astype(jnp.int32).reshape(1)
    group = a_log.shape[0]
    gains = lax.all_gather(jnp.stack([a_log, d_skip]), "head", tiled=True)
    skip = jnp.broadcast_to(gains[1::2].reshape(HEADS, 1), (HEADS, DIM)).reshape(1, WIDTH)
    raw_t = dt_raw.T
    pay, scal, cum2, half, rate, seg = states(
        place, raw_t, gains, seg_ids.reshape(-1, 128), inputs, cotangent, b_proj, c_proj
    )
    pay = lax.all_to_all(pay, everyone, 0, 0, tiled=True)
    ymix, dxmix, cpart, ddt, dbmix, dcmix, dskip = mix(
        inputs, cotangent, b_proj, c_proj, seg, skip, cum2, half
    )
    state = lax.all_to_all(scan(pay), everyone, 0, 0, tiled=True)
    raw_grad, sums = gradient_sums(
        inputs, cotangent, state, b_proj, c_proj, scal, raw_t, rate, cpart, ddt, dskip
    )
    sums = lax.all_to_all(sums.reshape(PARTS, 1, 128), everyone, 0, 0, tiled=True)
    y, dx, db, dc = finish(
        inputs, cotangent, ymix, dxmix, state, b_proj, c_proj, half, dbmix, dcmix
    )
    sums = jnp.sum(sums, axis=(0, 1))
    a_grad = lax.dynamic_slice(sums, (mine * group,), (group,))
    skip_grad = lax.dynamic_slice(sums, (HEADS + mine * group,), (group,))
    return (y, dx, raw_grad.T, db, dc, a_grad, skip_grad)


def solution(mesh):
    tokens = P(("seq", "head"), None)
    in_specs = (tokens, tokens, tokens, tokens, P("head"), P("head"), P("seq"), tokens)
    out_specs = (tokens, tokens, tokens, tokens, tokens, P("head"), P("head"))
    return jax.shard_map(body, mesh=mesh, in_specs=in_specs, out_specs=out_specs, check_vma=False)
```

```python
import jax
import jax.numpy as jnp
from jax import lax
from jax.experimental import pallas as pl
from jax.experimental.pallas import tpu as pltpu
from jax.sharding import PartitionSpec as P

HEADS = 64
DIM = 64
STATE = 128
BLOCK = 256
WIDTH = HEADS * DIM
PARTS = 128
PIECE = STATE * WIDTH // (PARTS * 128)
ROWS = STATE // PIECE
CARRY = 2 * PIECE
META = 8
LOG2E = 1.4426950408889634
F32 = jnp.float32
BF16 = jnp.bfloat16


def dot(a, b):
    return jnp.dot(a, b, preferred_element_type=F32)


def dot_nt(a, b):
    return lax.dot_general(a, b, (((1,), (1,)), ((), ())), preferred_element_type=F32)


def dot_tn(a, b):
    return lax.dot_general(a, b, (((0,), (0,)), ((), ())), preferred_element_type=F32)


def iota(shape, axis):
    return lax.broadcasted_iota(jnp.int32, shape, axis)


def ones_where(mask):
    return jnp.where(mask, 1.0, 0.0).astype(BF16)


def split2(value):
    high = value.astype(BF16)
    return high, (value - high.astype(F32)).astype(BF16)


def split3(value):
    high = value.astype(BF16)
    return (high,) + split2(value - high.astype(F32))


def spread(head0, lanes):
    shape = (2 * HEADS, lanes)
    return ones_where((iota(shape, 0) & (HEADS - 1)) == (iota(shape, 1) >> 6) + head0)


def gather_heads(head0, lanes, period):
    shape = (lanes, HEADS)
    return ones_where(((iota(shape, 0) & (period - 1)) >> 6) + head0 == iota(shape, 1))


def whole(*shape):
    return pl.BlockSpec(shape, lambda *_: (0,) * len(shape))


def wide(lanes):
    return pl.BlockSpec((BLOCK, lanes), lambda i: (0, i))


def pieces(lanes, rows):
    return pl.BlockSpec((PARTS * lanes // WIDTH, rows, 128), lambda i: (i, 0, 0))


def params(mib=60):
    return pltpu.CompilerParams(vmem_limit_bytes=mib * 1024 * 1024)


def cost(flops, moved, exps):
    return pl.CostEstimate(flops=flops, bytes_accessed=moved, transcendentals=exps)


def like(shape, kind=F32):
    return jax.ShapeDtypeStruct(shape, kind)


STATES_LANES = 2048


def states_kernel(
    place_ref, raw_ref, gains_ref, seg_ref, x_ref, g_ref, b_ref, c_ref,
    pay_ref, scal_ref, cum2_ref, half_ref, rate_ref, row_ref,
    bt_ref, ct_ref, meta_ref,
):
    step = pl.program_id(0)

    @pl.when(step == 0)
    def _():
        raw = raw_ref[...].astype(F32)
        dt = jnp.maximum(raw, 0.0) + jnp.log1p(jnp.exp(-jnp.abs(raw)))
        square = (BLOCK, BLOCK)
        upto = ones_where(iota(square, 0) <= iota(square, 1))
        high, mid, low = split3(dt)
        sums = dot(high, upto) + dot(mid, upto) + dot(low, upto)
        gains = gains_ref[...]
        alog = jnp.concatenate([gains[k : k + 1] for k in range(0, gains.shape[0], 2)], axis=1)
        rate = jnp.exp(jnp.broadcast_to(alog, (128, HEADS)).T)
        cum = -rate[:, :1] * sums
        tot = cum[:, BLOCK - 1 :]
        block = 2 * (place_ref[0] % (seg_ref.shape[0] // 2))
        seg = jnp.concatenate(
            [seg_ref[pl.ds(block, 1), :], seg_ref[pl.ds(block + 1, 1), :]], axis=1
        ).astype(F32)
        first, last = seg[:, :1], seg[:, BLOCK - 1 :]
        end = jnp.where(seg == last, jnp.exp(tot - cum), 0.0)
        start = jnp.where(seg == first, jnp.exp(cum), 0.0)
        weight = end * dt
        scal_ref[0] = end
        scal_ref[1] = weight
        scal_ref[2] = start
        scal_ref[3] = dt
        cum2_ref[...] = cum * LOG2E
        half_ref[0] = jnp.concatenate(split2(weight), axis=0).T
        half_ref[1] = jnp.concatenate(split2(start), axis=0).T
        half_ref[2] = jnp.concatenate(split2(dt), axis=0).T
        rate_ref[...] = rate
        row_ref[...] = seg
        bt_ref[...] = b_ref[...].T
        ct_ref[...] = c_ref[...].T
        kind = iota((HEADS, 128), 1)
        columns = jnp.zeros((HEADS, 128), F32)
        for k, part in enumerate(split3(tot)):
            columns = jnp.where(kind == k, part.astype(F32), columns)
        columns = jnp.where(kind == 3, first, jnp.where(kind == 4, last, columns))
        rows = jnp.concatenate([columns, jnp.zeros((HEADS, 128), F32)], axis=0).T
        meta_ref[...] = rows[:16].astype(BF16)

    copy = spread(step * (STATES_LANES // DIM), STATES_LANES)
    meta = dot(meta_ref[...], copy)[:META].astype(BF16)
    x_weighted = (x_ref[...].astype(F32) * dot(half_ref[0], copy)).astype(BF16)
    contrib = dot(bt_ref[...], x_weighted).astype(BF16)
    g_scaled = (g_ref[...].astype(F32) * dot(half_ref[1], copy)).astype(BF16)
    dh_low = dot(ct_ref[...], g_scaled).astype(BF16)
    for j in range(STATES_LANES // 128):
        lanes = slice(j * 128, (j + 1) * 128)
        for r in range(ROWS):
            rows = slice(r * PIECE, (r + 1) * PIECE)
            pay_ref[j * ROWS + r, :PIECE, :] = contrib[rows, lanes]
            pay_ref[j * ROWS + r, PIECE:CARRY, :] = dh_low[rows, lanes]
            pay_ref[j * ROWS + r, CARRY:, :] = meta[:, lanes]


def states(place, raw_t, gains, seg_ids, x, g, b, c):
    return pl.pallas_call(
        states_kernel,
        grid=(WIDTH // STATES_LANES,),
        in_specs=[
            pl.BlockSpec(memory_space=pltpu.SMEM),
            whole(HEADS, BLOCK), whole(*gains.shape), whole(*seg_ids.shape),
            wide(STATES_LANES), wide(STATES_LANES), whole(BLOCK, STATE), whole(BLOCK, STATE),
        ],
        out_specs=[
            pieces(STATES_LANES, CARRY + META), whole(4, HEADS, BLOCK), whole(HEADS, BLOCK),
            whole(3, BLOCK, 2 * HEADS), whole(HEADS, 128), whole(1, BLOCK),
        ],
        out_shape=[
            like((PARTS, CARRY + META, 128), BF16), like((4, HEADS, BLOCK)), like((HEADS, BLOCK)),
            like((3, BLOCK, 2 * HEADS), BF16), like((HEADS, 128)), like((1, BLOCK)),
        ],
        scratch_shapes=[
            pltpu.VMEM((STATE, BLOCK), BF16),
            pltpu.VMEM((STATE, BLOCK), BF16),
            pltpu.VMEM((16, 2 * HEADS), BF16),
        ],
        compiler_params=params(),
        cost_estimate=cost(10**9, 8 * 10**6, 10**5),
        name="states",
    )(place, raw_t, gains, seg_ids, x, g, b, c)


MIX_LANES = 512


def mix_kernel(
    x_ref, g_ref, b_ref, c_ref, seg_ref, skip_ref, cum2_ref, half_ref,
    y_ref, dx_ref, cpart_ref, ddt_ref, db_ref, dc_ref, dskip_ref,
    gram_ref, mask_ref, total_ref, cpart_sum_ref, ddt_sum_ref, dskip_sum_ref,
):
    step = pl.program_id(0)
    square = (BLOCK, BLOCK)

    @pl.when(step == 0)
    def _():
        seg_row = seg_ref[...]
        seg_col = jnp.broadcast_to(seg_row, square).T
        keep = (seg_row == seg_col) & (iota(square, 0) >= iota(square, 1))
        mask_ref[...] = jnp.where(keep, 0.0, -1e30)
        gram_ref[...] = dot_nt(c_ref[...], b_ref[...])
        total_ref[...] = jnp.zeros_like(total_ref)
        cpart_sum_ref[...] = jnp.zeros_like(cpart_sum_ref)
        ddt_sum_ref[...] = jnp.zeros_like(ddt_sum_ref)
        dskip_sum_ref[...] = jnp.zeros_like(dskip_sum_ref)

    lower = iota((BLOCK, 128), 1) < DIM
    zero = jnp.zeros((BLOCK, 128), BF16)
    cum2 = cum2_ref[...]
    columns = cum2.T
    for j in range(MIX_LANES // 128):
        head0 = step * (MIX_LANES // DIM) + 2 * j
        lanes = slice(j * 128, (j + 1) * 128)
        x_low = x_ref[:, lanes]
        g_low = g_ref[:, lanes]
        x = x_low.astype(F32)
        g = g_low.astype(F32)
        dt = dot(half_ref[2], spread(head0, 128))
        x_dt = (x * dt).astype(BF16)
        y = jnp.zeros((BLOCK, 128), F32)
        dx = jnp.zeros((BLOCK, 128), F32)
        for k in range(2):
            pick = lower if k == 0 else ~lower
            g_one = jnp.where(pick, g_low, zero)
            x_one = jnp.where(pick, x_dt, zero)
            head = 2 * j + k
            gap = columns[:, head : head + 1] - cum2[head : head + 1, :]
            kern = jnp.exp2(gap + mask_ref[...])
            mixed = (gram_ref[...] * kern).astype(BF16)
            total_ref[...] += dot_nt(g_one, x_dt) * kern
            y += dot(mixed, x_one)
            dx += dot_tn(mixed, g_one)
        skip = skip_ref[:, lanes]
        gather = gather_heads(head0, 256, 128)
        y_ref[:, lanes] = (y + skip * x).astype(BF16)
        dx_ref[:, lanes] = (dx * dt + skip * g).astype(BF16)
        apart = jnp.concatenate(split2(g * y - x_dt.astype(F32) * dx), axis=1)
        cpart_sum_ref[...] += dot(apart, gather)
        ddt_sum_ref[...] += dot((x * dx).astype(BF16), gather[:128])
        channel_sum = jnp.broadcast_to(jnp.sum(g * x, axis=0, keepdims=True), (8, 128))
        dskip_sum_ref[...] += dot(jnp.concatenate(split2(channel_sum), axis=1), gather)

    @pl.when(step == WIDTH // MIX_LANES - 1)
    def _():
        total = total_ref[...].astype(BF16)
        dc_ref[...] = dot(total, b_ref[...])
        db_ref[...] = dot_tn(total, c_ref[...])
        cpart_ref[...] = cpart_sum_ref[...].T
        ddt_ref[...] = ddt_sum_ref[...].T
        dskip_ref[...] = jnp.broadcast_to(dskip_sum_ref[:1], (128, HEADS)).T


def mix(x, g, b, c, seg, skip, cum2, half):
    return pl.pallas_call(
        mix_kernel,
        grid=(WIDTH // MIX_LANES,),
        in_specs=[
            wide(MIX_LANES), wide(MIX_LANES), whole(BLOCK, STATE), whole(BLOCK, STATE),
            whole(1, BLOCK),
            pl.BlockSpec((1, MIX_LANES), lambda i: (0, i)),
            pl.BlockSpec((MIX_LANES // DIM, BLOCK), lambda i: (i, 0)),
            whole(3, BLOCK, 2 * HEADS),
        ],
        out_specs=[
            wide(MIX_LANES), wide(MIX_LANES), whole(HEADS, BLOCK), whole(HEADS, BLOCK),
            whole(BLOCK, STATE), whole(BLOCK, STATE), whole(HEADS, 128),
        ],
        out_shape=[
            like((BLOCK, WIDTH), BF16), like((BLOCK, WIDTH), BF16),
            like((HEADS, BLOCK)), like((HEADS, BLOCK)),
            like((BLOCK, STATE)), like((BLOCK, STATE)), like((HEADS, 128)),
        ],
        scratch_shapes=[pltpu.VMEM((BLOCK, BLOCK), F32)] * 3
        + [pltpu.VMEM((BLOCK, HEADS), F32)] * 2
        + [pltpu.VMEM((8, HEADS), F32)],
        compiler_params=params(),
        cost_estimate=cost(20 * 10**9, 9 * 10**6, 4 * 10**6),
        name="mix",
    )(x, g, b, c, seg, skip, cum2, half)


def scan_kernel(pay_ref, out_ref):
    square = (PARTS, PARTS)
    notes = jnp.swapaxes(pay_ref[:, CARRY:, :].astype(F32), 0, 1)
    high, mid, low, first, last = (notes[k] for k in range(5))
    upto = ones_where(iota(square, 0) >= iota(square, 1))
    through = dot(upto, high.astype(BF16)) + dot(upto, mid.astype(BF16)) + dot(upto, low.astype(BF16))
    ahead = through - (high + mid + low)
    through_t = through.T
    keep = (iota(square, 0) > iota(square, 1)) & (first[:, :1] == last.T[:1, :])
    forward, backward = [], []
    for lane in (0, DIM):
        gap = ahead[:, lane : lane + 1] - through_t[lane : lane + 1, :]
        carry = jnp.where(keep, jnp.exp(jnp.minimum(gap, 0.0)), 0.0)
        forward.append(carry.astype(BF16))
        backward.append(carry.T.astype(BF16))
    forward = jnp.concatenate(forward, axis=0)
    backward = jnp.concatenate(backward, axis=0)
    lower = iota((PARTS, 256), 1) & (128 - 1) < DIM

    for k in range(0, CARRY, 16):
        block = jnp.swapaxes(pay_ref[:, k : k + 16, :], 0, 1)
        done = []
        for i in range(0, 16, 2):
            rows = jnp.concatenate([block[i], block[i + 1]], axis=1)
            both = dot(forward if k < PIECE else backward, rows)
            pair = jnp.where(lower, both[:PARTS], both[PARTS:]).astype(BF16)
            done += [pair[:, :128], pair[:, 128:]]
        out_ref[:, k : k + 16, :] = jnp.swapaxes(jnp.stack(done), 0, 1)


def scan(pay):
    return pl.pallas_call(
        scan_kernel,
        out_shape=like((PARTS, CARRY, 128), BF16),
        in_specs=[pl.BlockSpec(memory_space=pltpu.VMEM)],
        out_specs=pl.BlockSpec(memory_space=pltpu.VMEM),
        compiler_params=params(16),
        cost_estimate=cost(5 * 10**8, 5 * 10**6, 10**5),
        name="scan",
    )(pay)


def carried(state_ref, j):
    tiles = [state_ref[k * ROWS : (k + 1) * ROWS] for k in (2 * j, 2 * j + 1)]
    h_low = jnp.concatenate([tile[:, :PIECE].reshape(STATE, 128) for tile in tiles], axis=1)
    lam_low = jnp.concatenate([tile[:, PIECE:].reshape(STATE, 128) for tile in tiles], axis=1)
    return h_low, lam_low


SUMS_LANES = 2048


def sums_kernel(
    x_ref, g_ref, state_ref, b_ref, c_ref, scal_ref, raw_ref, rate_ref,
    cpart_ref, ddt_ref, dskip_ref,
    raw_grad_ref, sums_ref,
    dstart_ref, dweight_ref, ddecay_ref,
):
    step = pl.program_id(0)

    @pl.when(step == 0)
    def _():
        dstart_ref[...] = jnp.zeros_like(dstart_ref)
        dweight_ref[...] = jnp.zeros_like(dweight_ref)
        ddecay_ref[...] = jnp.zeros_like(ddecay_ref)

    for j in range(SUMS_LANES // 256):
        lanes = slice(j * 256, (j + 1) * 256)
        gather = gather_heads(step * (SUMS_LANES // DIM) + 4 * j, 256, 256)
        h_low, lam_low = carried(state_ref, j)
        from_state = dot(c_ref[...], h_low)
        from_grad = dot(b_ref[...], lam_low)
        dstart_ref[...] += dot((g_ref[:, lanes].astype(F32) * from_state).astype(BF16), gather)
        dweight_ref[...] += dot((x_ref[:, lanes].astype(F32) * from_grad).astype(BF16), gather)
        ddecay_ref[...] += dot((h_low.astype(F32) * lam_low.astype(F32)).astype(BF16), gather)

    @pl.when(step == WIDTH // SUMS_LANES - 1)
    def _():
        end, weight, start, dt = (scal_ref[k] for k in range(4))
        d_weight = dweight_ref[...].T
        used = d_weight * weight
        d_cum = cpart_ref[...] + dstart_ref[...].T * start - used
        at_last = iota((HEADS, BLOCK), 1) == BLOCK - 1
        d_decay = jnp.sum(ddecay_ref[...].T, axis=1, keepdims=True)
        d_total = jnp.sum(used, axis=1, keepdims=True) + d_decay * start[:, BLOCK - 1 :]
        d_cum = d_cum + jnp.where(at_last, d_total, 0.0)
        square = (BLOCK, BLOCK)
        onward = ones_where(iota(square, 0) >= iota(square, 1))
        high, mid, low = split3(d_cum)
        d_log = dot(high, onward) + dot(mid, onward) + dot(low, onward)
        rate = rate_ref[:, :1]
        d_dt = ddt_ref[...] + d_weight * end - rate * d_log
        raw = raw_ref[...].astype(F32)
        raw_grad_ref[...] = (d_dt / (1.0 + jnp.exp(-raw))).astype(BF16)
        rate_grad = -jnp.sum(dt * d_log, axis=1, keepdims=True) * rate
        column = jnp.concatenate([rate_grad, dskip_ref[:, :1]], axis=0)
        sums_ref[...] = jnp.broadcast_to(column, (PARTS, 128)).T


def gradient_sums(x, g, state, b, c, scal, raw_t, rate, cpart, ddt, dskip):
    return pl.pallas_call(
        sums_kernel,
        grid=(WIDTH // SUMS_LANES,),
        in_specs=[
            wide(SUMS_LANES), wide(SUMS_LANES), pieces(SUMS_LANES, CARRY),
            whole(BLOCK, STATE), whole(BLOCK, STATE),
            whole(4, HEADS, BLOCK), whole(HEADS, BLOCK), whole(HEADS, 128),
            whole(HEADS, BLOCK), whole(HEADS, BLOCK), whole(HEADS, 128),
        ],
        out_specs=[whole(HEADS, BLOCK), whole(PARTS, 128)],
        out_shape=[like((HEADS, BLOCK), BF16), like((PARTS, 128))],
        scratch_shapes=[
            pltpu.VMEM((BLOCK, HEADS), F32),
            pltpu.VMEM((BLOCK, HEADS), F32),
            pltpu.VMEM((STATE, HEADS), F32),
        ],
        compiler_params=params(),
        cost_estimate=cost(10**9, 8 * 10**6, 10**5),
        name="gradient_sums",
    )(x, g, state, b, c, scal, raw_t, rate, cpart, ddt, dskip)


FINISH_LANES = 1024


def finish_kernel(
    x_ref, g_ref, ymix_ref, dxmix_ref, state_ref, b_ref, c_ref, half_ref, dbmix_ref, dcmix_ref,
    y_ref, dx_ref, db_ref, dc_ref,
):
    step = pl.program_id(0)

    @pl.when(step == 0)
    def _():
        db_ref[...] = dbmix_ref[...]
        dc_ref[...] = dcmix_ref[...]

    for j in range(FINISH_LANES // 256):
        copy = spread(step * (FINISH_LANES // DIM) + 4 * j, 256)
        lanes = slice(j * 256, (j + 1) * 256)
        x = x_ref[:, lanes].astype(F32)
        g = g_ref[:, lanes].astype(F32)
        h_low, lam_low = carried(state_ref, j)
        weight = dot(half_ref[0], copy)
        start = dot(half_ref[1], copy)
        from_state = dot(c_ref[...], h_low)
        from_grad = dot(b_ref[...], lam_low)
        y_ref[:, lanes] = (ymix_ref[:, lanes].astype(F32) + start * from_state).astype(BF16)
        dx_ref[:, lanes] = (dxmix_ref[:, lanes].astype(F32) + weight * from_grad).astype(BF16)
        dc_ref[...] += dot_nt((start * g).astype(BF16), h_low)
        db_ref[...] += dot_nt((weight * x).astype(BF16), lam_low)


def finish(x, g, ymix, dxmix, state, b, c, half, dbmix, dcmix):
    lanes = FINISH_LANES
    return pl.pallas_call(
        finish_kernel,
        grid=(WIDTH // lanes,),
        in_specs=[
            wide(lanes), wide(lanes), wide(lanes), wide(lanes), pieces(lanes, CARRY),
            whole(BLOCK, STATE), whole(BLOCK, STATE),
            whole(3, BLOCK, 2 * HEADS), whole(BLOCK, STATE), whole(BLOCK, STATE),
        ],
        out_specs=[wide(lanes), wide(lanes), whole(BLOCK, STATE), whole(BLOCK, STATE)],
        out_shape=[
            like((BLOCK, WIDTH), BF16), like((BLOCK, WIDTH), BF16),
            like((BLOCK, STATE)), like((BLOCK, STATE)),
        ],
        compiler_params=params(),
        cost_estimate=cost(8 * 10**9, 16 * 10**6, 10**5),
        name="finish",
    )(x, g, ymix, dxmix, state, b, c, half, dbmix, dcmix)


def body(inputs, dt_raw, b_proj, c_proj, a_log, d_skip, seg_ids, cotangent):
    everyone = ("seq", "head")
    mine = lax.axis_index("head")
    place = mine.astype(jnp.int32).reshape(1)
    group = a_log.shape[0]
    gains = lax.all_gather(jnp.stack([a_log, d_skip]), "head", tiled=True)
    skip = jnp.broadcast_to(gains[1::2].reshape(HEADS, 1), (HEADS, DIM)).reshape(1, WIDTH)
    raw_t = dt_raw.T
    pay, scal, cum2, half, rate, seg = states(
        place, raw_t, gains, seg_ids.reshape(-1, 128), inputs, cotangent, b_proj, c_proj
    )
    pay = lax.all_to_all(pay, everyone, 0, 0, tiled=True)
    ymix, dxmix, cpart, ddt, dbmix, dcmix, dskip = mix(
        inputs, cotangent, b_proj, c_proj, seg, skip, cum2, half
    )
    state = lax.all_to_all(scan(pay), everyone, 0, 0, tiled=True)
    raw_grad, sums = gradient_sums(
        inputs, cotangent, state, b_proj, c_proj, scal, raw_t, rate, cpart, ddt, dskip
    )
    sums = lax.all_to_all(sums.reshape(PARTS, 1, 128), everyone, 0, 0, tiled=True)
    y, dx, db, dc = finish(
        inputs, cotangent, ymix, dxmix, state, b_proj, c_proj, half, dbmix, dcmix
    )
    sums = jnp.sum(sums, axis=(0, 1))
    a_grad = lax.dynamic_slice(sums, (mine * group,), (group,))
    skip_grad = lax.dynamic_slice(sums, (HEADS + mine * group,), (group,))
    return (y, dx, raw_grad.T, db, dc, a_grad, skip_grad)


def solution(mesh):
    tokens = P(("seq", "head"), None)
    in_specs = (tokens, tokens, tokens, tokens, P("head"), P("head"), P("seq"), tokens)
    out_specs = (tokens, tokens, tokens, tokens, tokens, P("head"), P("head"))
    return jax.shard_map(body, mesh=mesh, in_specs=in_specs, out_specs=out_specs, check_vma=False)
```

```python
import jax
import jax.numpy as jnp
from jax import lax
from jax.experimental import pallas as pl
from jax.experimental.pallas import tpu as pltpu
from jax.sharding import PartitionSpec as P

HEADS = 64
DIM = 64
STATE = 128
BLOCK = 256
WIDTH = HEADS * DIM
PARTS = 128
PIECE = STATE * WIDTH // (PARTS * 128)
ROWS = STATE // PIECE
CARRY = 2 * PIECE
META = 8
LOG2E = 1.4426950408889634
F32 = jnp.float32
BF16 = jnp.bfloat16


def dot(a, b):
    return jnp.dot(a, b, preferred_element_type=F32)


def dot_nt(a, b):
    return lax.dot_general(a, b, (((1,), (1,)), ((), ())), preferred_element_type=F32)


def dot_tn(a, b):
    return lax.dot_general(a, b, (((0,), (0,)), ((), ())), preferred_element_type=F32)


def iota(shape, axis):
    return lax.broadcasted_iota(jnp.int32, shape, axis)


def ones_where(mask):
    return jnp.where(mask, 1.0, 0.0).astype(BF16)


def split2(value):
    high = value.astype(BF16)
    return high, (value - high.astype(F32)).astype(BF16)


def split3(value):
    high = value.astype(BF16)
    return (high,) + split2(value - high.astype(F32))


def spread(head0, lanes):
    shape = (2 * HEADS, lanes)
    return ones_where((iota(shape, 0) & (HEADS - 1)) == (iota(shape, 1) >> 6) + head0)


def gather_heads(head0, lanes, period):
    shape = (lanes, HEADS)
    return ones_where(((iota(shape, 0) & (period - 1)) >> 6) + head0 == iota(shape, 1))


def whole(*shape):
    return pl.BlockSpec(shape, lambda *_: (0,) * len(shape))


def wide(lanes):
    return pl.BlockSpec((BLOCK, lanes), lambda i: (0, i))


def pieces(lanes, rows):
    return pl.BlockSpec((PARTS * lanes // WIDTH, rows, 128), lambda i: (i, 0, 0))


def params(mib=62):
    return pltpu.CompilerParams(vmem_limit_bytes=mib * 1024 * 1024)


def cost(flops, moved, exps):
    return pl.CostEstimate(flops=flops, bytes_accessed=moved, transcendentals=exps)


def like(shape, kind=F32):
    return jax.ShapeDtypeStruct(shape, kind)


STATES_LANES = 2048


def heads_row(gains, row):
    return jnp.concatenate([gains[k : k + 1] for k in range(row, gains.shape[0], 2)], axis=1)


def states_kernel(
    place_ref, raw_ref, gains_ref, seg_ref, x_ref, g_ref, b_ref, c_ref,
    pay_ref, scal_ref, cum2_ref, half_ref, rate_ref, row_ref, skip_ref,
    bt_ref, ct_ref, meta_ref,
):
    step = pl.program_id(0)

    @pl.when(step == 0)
    def _():
        raw = raw_ref[...].astype(F32)
        dt = jnp.maximum(raw, 0.0) + jnp.log1p(jnp.exp(-jnp.abs(raw)))
        square = (BLOCK, BLOCK)
        upto = ones_where(iota(square, 0) <= iota(square, 1))
        high, mid, low = split3(dt)
        sums = dot(high, upto) + dot(mid, upto) + dot(low, upto)
        gains = gains_ref[...]
        alog = heads_row(gains, 0)
        skip = jnp.broadcast_to(heads_row(gains, 1), (16, HEADS))
        skip_ref[...] = jnp.concatenate(split2(skip), axis=1)
        rate = jnp.exp(jnp.broadcast_to(alog, (128, HEADS)).T)
        cum = -rate[:, :1] * sums
        tot = cum[:, BLOCK - 1 :]
        block = 2 * (place_ref[0] % (seg_ref.shape[0] // 2))
        seg = jnp.concatenate(
            [seg_ref[pl.ds(block, 1), :], seg_ref[pl.ds(block + 1, 1), :]], axis=1
        ).astype(F32)
        first, last = seg[:, :1], seg[:, BLOCK - 1 :]
        end = jnp.where(seg == last, jnp.exp(tot - cum), 0.0)
        start = jnp.where(seg == first, jnp.exp(cum), 0.0)
        weight = end * dt
        scal_ref[0] = end
        scal_ref[1] = weight
        scal_ref[2] = start
        scal_ref[3] = cum
        cum2_ref[...] = cum * LOG2E
        half_ref[0] = jnp.concatenate(split2(weight), axis=0).T
        half_ref[1] = jnp.concatenate(split2(start), axis=0).T
        half_ref[2] = jnp.concatenate(split2(dt), axis=0).T
        rate_ref[...] = rate
        row_ref[...] = seg
        bt_ref[...] = b_ref[...].T
        ct_ref[...] = c_ref[...].T
        kind = iota((HEADS, 128), 1)
        columns = jnp.zeros((HEADS, 128), F32)
        for k, part in enumerate(split3(tot)):
            columns = jnp.where(kind == k, part.astype(F32), columns)
        columns = jnp.where(kind == 3, first, jnp.where(kind == 4, last, columns))
        rows = jnp.concatenate([columns, jnp.zeros((HEADS, 128), F32)], axis=0).T
        meta_ref[...] = rows[:16].astype(BF16)

    copy = spread(step * (STATES_LANES // DIM), STATES_LANES)
    meta = dot(meta_ref[...], copy)[:META].astype(BF16)
    x_weighted = (x_ref[...].astype(F32) * dot(half_ref[0], copy)).astype(BF16)
    contrib = dot(bt_ref[...], x_weighted).astype(BF16)
    g_scaled = (g_ref[...].astype(F32) * dot(half_ref[1], copy)).astype(BF16)
    dh_low = dot(ct_ref[...], g_scaled).astype(BF16)
    for j in range(STATES_LANES // 128):
        lanes = slice(j * 128, (j + 1) * 128)
        for r in range(ROWS):
            rows = slice(r * PIECE, (r + 1) * PIECE)
            pay_ref[j * ROWS + r, :PIECE, :] = contrib[rows, lanes]
            pay_ref[j * ROWS + r, PIECE:CARRY, :] = dh_low[rows, lanes]
            pay_ref[j * ROWS + r, CARRY:, :] = meta[:, lanes]


def states(place, raw_t, gains, seg_ids, x, g, b, c):
    return pl.pallas_call(
        states_kernel,
        grid=(WIDTH // STATES_LANES,),
        in_specs=[
            pl.BlockSpec(memory_space=pltpu.SMEM),
            whole(HEADS, BLOCK), whole(*gains.shape), whole(*seg_ids.shape),
            wide(STATES_LANES), wide(STATES_LANES), whole(BLOCK, STATE), whole(BLOCK, STATE),
        ],
        out_specs=[
            pieces(STATES_LANES, CARRY + META), whole(4, HEADS, BLOCK), whole(HEADS, BLOCK),
            whole(3, BLOCK, 2 * HEADS), whole(HEADS, 128), whole(1, BLOCK), whole(16, 2 * HEADS),
        ],
        out_shape=[
            like((PARTS, CARRY + META, 128), BF16), like((4, HEADS, BLOCK)), like((HEADS, BLOCK)),
            like((3, BLOCK, 2 * HEADS), BF16), like((HEADS, 128)), like((1, BLOCK)),
            like((16, 2 * HEADS), BF16),
        ],
        scratch_shapes=[
            pltpu.VMEM((STATE, BLOCK), BF16),
            pltpu.VMEM((STATE, BLOCK), BF16),
            pltpu.VMEM((16, 2 * HEADS), BF16),
        ],
        compiler_params=params(),
        cost_estimate=cost(10**9, 8 * 10**6, 10**5),
        name="states",
    )(place, raw_t, gains, seg_ids, x, g, b, c)


MIX_LANES = 512


def mix_kernel(
    x_ref, g_ref, b_ref, c_ref, seg_ref, skip_ref, cum2_ref, half_ref,
    y_ref, dx_ref, cpart_ref, ddt_ref, db_ref, dc_ref, dskip_ref,
    gram_ref, mask_ref, total_ref, cpart_sum_ref, ddt_sum_ref, dskip_sum_ref,
):
    step = pl.program_id(0)
    square = (BLOCK, BLOCK)

    @pl.when(step == 0)
    def _():
        seg_row = seg_ref[...]
        seg_col = jnp.broadcast_to(seg_row, square).T
        keep = (seg_row == seg_col) & (iota(square, 0) >= iota(square, 1))
        mask_ref[...] = jnp.where(keep, 0.0, -1e30)
        gram_ref[...] = dot_nt(c_ref[...], b_ref[...])
        total_ref[...] = jnp.zeros_like(total_ref)
        cpart_sum_ref[...] = jnp.zeros_like(cpart_sum_ref)
        ddt_sum_ref[...] = jnp.zeros_like(ddt_sum_ref)
        dskip_sum_ref[...] = jnp.zeros_like(dskip_sum_ref)

    lower = iota((BLOCK, 128), 1) < DIM
    zero = jnp.zeros((BLOCK, 128), BF16)
    cum2 = cum2_ref[...]
    columns = cum2.T
    for j in range(MIX_LANES // 128):
        head0 = step * (MIX_LANES // DIM) + 2 * j
        lanes = slice(j * 128, (j + 1) * 128)
        x_low = x_ref[:, lanes]
        g_low = g_ref[:, lanes]
        x = x_low.astype(F32)
        g = g_low.astype(F32)
        copy = spread(head0, 128)
        dt = dot(half_ref[2], copy)
        x_dt = (x * dt).astype(BF16)
        y = jnp.zeros((BLOCK, 128), F32)
        dx = jnp.zeros((BLOCK, 128), F32)
        for k in range(2):
            pick = lower if k == 0 else ~lower
            g_one = jnp.where(pick, g_low, zero)
            x_one = jnp.where(pick, x_dt, zero)
            head = 2 * j + k
            gap = columns[:, head : head + 1] - cum2[head : head + 1, :]
            kern = jnp.exp2(gap + mask_ref[...])
            mixed = (gram_ref[...] * kern).astype(BF16)
            total_ref[...] += dot_nt(g_one, x_dt) * kern
            y += dot(mixed, x_one)
            dx += dot_tn(mixed, g_one)
        skip = dot(skip_ref[...], copy)[:1]
        gather = gather_heads(head0, 256, 128)
        y_ref[:, lanes] = (y + skip * x).astype(BF16)
        dx_ref[:, lanes] = (dx * dt + skip * g).astype(BF16)
        apart = jnp.concatenate(split2(g * y - x_dt.astype(F32) * dx), axis=1)
        cpart_sum_ref[...] += dot(apart, gather)
        ddt_sum_ref[...] += dot((x * dx).astype(BF16), gather[:128])
        channel_sum = jnp.broadcast_to(jnp.sum(g * x, axis=0, keepdims=True), (8, 128))
        dskip_sum_ref[...] += dot(jnp.concatenate(split2(channel_sum), axis=1), gather)

    @pl.when(step == WIDTH // MIX_LANES - 1)
    def _():
        total = total_ref[...].astype(BF16)
        dc_ref[...] = dot(total, b_ref[...])
        db_ref[...] = dot_tn(total, c_ref[...])
        cpart_ref[...] = cpart_sum_ref[...].T
        ddt_ref[...] = ddt_sum_ref[...].T
        dskip_ref[...] = jnp.broadcast_to(dskip_sum_ref[:1], (128, HEADS)).T


def mix(x, g, b, c, seg, skip, cum2, half):
    return pl.pallas_call(
        mix_kernel,
        grid=(WIDTH // MIX_LANES,),
        in_specs=[
            wide(MIX_LANES), wide(MIX_LANES), whole(BLOCK, STATE), whole(BLOCK, STATE),
            whole(1, BLOCK),
            whole(16, 2 * HEADS),
            pl.BlockSpec((MIX_LANES // DIM, BLOCK), lambda i: (i, 0)),
            whole(3, BLOCK, 2 * HEADS),
        ],
        out_specs=[
            wide(MIX_LANES), wide(MIX_LANES), whole(HEADS, BLOCK), whole(HEADS, BLOCK),
            whole(BLOCK, STATE), whole(BLOCK, STATE), whole(HEADS, 128),
        ],
        out_shape=[
            like((BLOCK, WIDTH), BF16), like((BLOCK, WIDTH), BF16),
            like((HEADS, BLOCK)), like((HEADS, BLOCK)),
            like((BLOCK, STATE)), like((BLOCK, STATE)), like((HEADS, 128)),
        ],
        scratch_shapes=[pltpu.VMEM((BLOCK, BLOCK), F32)] * 3
        + [pltpu.VMEM((BLOCK, HEADS), F32)] * 2
        + [pltpu.VMEM((8, HEADS), F32)],
        compiler_params=params(),
        cost_estimate=cost(20 * 10**9, 9 * 10**6, 4 * 10**6),
        name="mix",
    )(x, g, b, c, seg, skip, cum2, half)


def scan_kernel(pay_ref, out_ref):
    square = (PARTS, PARTS)
    notes = jnp.swapaxes(pay_ref[:, CARRY:, :].astype(F32), 0, 1)
    high, mid, low, first, last = (notes[k] for k in range(5))
    upto = ones_where(iota(square, 0) >= iota(square, 1))
    through = dot(upto, high.astype(BF16)) + dot(upto, mid.astype(BF16)) + dot(upto, low.astype(BF16))
    ahead = through - (high + mid + low)
    through_t = through.T
    keep = (iota(square, 0) > iota(square, 1)) & (first[:, :1] == last.T[:1, :])
    forward, backward = [], []
    for lane in (0, DIM):
        gap = ahead[:, lane : lane + 1] - through_t[lane : lane + 1, :]
        carry = jnp.where(keep, jnp.exp(jnp.minimum(gap, 0.0)), 0.0)
        forward.append(carry.astype(BF16))
        backward.append(carry.T.astype(BF16))
    forward = jnp.concatenate(forward, axis=0)
    backward = jnp.concatenate(backward, axis=0)
    lower = iota((PARTS, 256), 1) & (128 - 1) < DIM

    for k in range(0, CARRY, 16):
        block = jnp.swapaxes(pay_ref[:, k : k + 16, :], 0, 1)
        done = []
        for i in range(0, 16, 2):
            rows = jnp.concatenate([block[i], block[i + 1]], axis=1)
            both = dot(forward if k < PIECE else backward, rows)
            pair = jnp.where(lower, both[:PARTS], both[PARTS:]).astype(BF16)
            done += [pair[:, :128], pair[:, 128:]]
        out_ref[:, k : k + 16, :] = jnp.swapaxes(jnp.stack(done), 0, 1)


def scan(pay):
    return pl.pallas_call(
        scan_kernel,
        out_shape=like((PARTS, CARRY, 128), BF16),
        in_specs=[pl.BlockSpec(memory_space=pltpu.VMEM)],
        out_specs=pl.BlockSpec(memory_space=pltpu.VMEM),
        compiler_params=params(16),
        cost_estimate=cost(5 * 10**8, 5 * 10**6, 10**5),
        name="scan",
    )(pay)


def carried(state_ref):
    tiles = [state_ref[k : k + ROWS] for k in range(0, state_ref.shape[0], ROWS)]
    h_low = jnp.concatenate([tile[:, :PIECE].reshape(STATE, 128) for tile in tiles], axis=1)
    lam_low = jnp.concatenate([tile[:, PIECE:].reshape(STATE, 128) for tile in tiles], axis=1)
    return h_low, lam_low


SUMS_LANES = 2048


def sums_kernel(
    x_ref, g_ref, state_ref, b_ref, c_ref, scal_ref, cpart_ref, dskip_ref,
    grads_ref, sums_ref,
    dstart_ref, dweight_ref, ddecay_ref,
):
    step = pl.program_id(0)

    @pl.when(step == 0)
    def _():
        dstart_ref[...] = jnp.zeros_like(dstart_ref)
        dweight_ref[...] = jnp.zeros_like(dweight_ref)
        ddecay_ref[...] = jnp.zeros_like(ddecay_ref)

    h_low, lam_low = carried(state_ref)
    start_terms, weight_terms = [], []
    for j in range(SUMS_LANES // 256):
        lanes = slice(j * 256, (j + 1) * 256)
        from_state = dot(c_ref[...], h_low[:, lanes])
        from_grad = dot(b_ref[...], lam_low[:, lanes])
        start_terms.append((g_ref[:, lanes].astype(F32) * from_state).astype(BF16))
        weight_terms.append((x_ref[:, lanes].astype(F32) * from_grad).astype(BF16))
    gather = gather_heads(step * (SUMS_LANES // DIM), SUMS_LANES, SUMS_LANES)
    dstart_ref[...] += dot(jnp.concatenate(start_terms, axis=1), gather)
    dweight_ref[...] += dot(jnp.concatenate(weight_terms, axis=1), gather)
    ddecay_ref[...] += dot((h_low.astype(F32) * lam_low.astype(F32)).astype(BF16), gather)

    @pl.when(step == WIDTH // SUMS_LANES - 1)
    def _():
        weight, start, cum = (scal_ref[k] for k in (1, 2, 3))
        d_weight = dweight_ref[...].T
        used = d_weight * weight
        d_cum = cpart_ref[...] + dstart_ref[...].T * start - used
        at_last = iota((HEADS, BLOCK), 1) == BLOCK - 1
        d_decay = jnp.sum(ddecay_ref[...].T, axis=1, keepdims=True)
        d_total = jnp.sum(used, axis=1, keepdims=True) + d_decay * start[:, BLOCK - 1 :]
        d_cum = d_cum + jnp.where(at_last, d_total, 0.0)
        grads_ref[0] = d_cum
        grads_ref[1] = d_weight
        rate_grad = jnp.sum(cum * d_cum, axis=1, keepdims=True)
        column = jnp.concatenate([rate_grad, dskip_ref[:, :1]], axis=0)
        sums_ref[...] = jnp.broadcast_to(column, (PARTS, 128)).T


def gradient_sums(x, g, state, b, c, scal, cpart, dskip):
    return pl.pallas_call(
        sums_kernel,
        grid=(WIDTH // SUMS_LANES,),
        in_specs=[
            wide(SUMS_LANES), wide(SUMS_LANES), pieces(SUMS_LANES, CARRY),
            whole(BLOCK, STATE), whole(BLOCK, STATE),
            whole(4, HEADS, BLOCK), whole(HEADS, BLOCK), whole(HEADS, 128),
        ],
        out_specs=[whole(2, HEADS, BLOCK), whole(PARTS, 128)],
        out_shape=[like((2, HEADS, BLOCK)), like((PARTS, 128))],
        scratch_shapes=[
            pltpu.VMEM((BLOCK, HEADS), F32),
            pltpu.VMEM((BLOCK, HEADS), F32),
            pltpu.VMEM((STATE, HEADS), F32),
        ],
        compiler_params=params(),
        cost_estimate=cost(10**9, 8 * 10**6, 10**5),
        name="gradient_sums",
    )(x, g, state, b, c, scal, cpart, dskip)


FINISH_LANES = 1024


def finish_kernel(
    x_ref, g_ref, ymix_ref, dxmix_ref, state_ref, b_ref, c_ref, half_ref, dbmix_ref, dcmix_ref,
    raw_ref, rate_ref, scal_ref, grads_ref, ddt_ref,
    y_ref, dx_ref, db_ref, dc_ref, raw_grad_ref,
):
    step = pl.program_id(0)

    @pl.when(step == 0)
    def _():
        db_ref[...] = dbmix_ref[...]
        dc_ref[...] = dcmix_ref[...]
        square = (BLOCK, BLOCK)
        onward = ones_where(iota(square, 0) >= iota(square, 1))
        high, mid, low = split3(grads_ref[0])
        d_log = dot(high, onward) + dot(mid, onward) + dot(low, onward)
        d_dt = ddt_ref[...] + grads_ref[1] * scal_ref[0] - rate_ref[:, :1] * d_log
        raw = raw_ref[...].astype(F32)
        raw_grad_ref[...] = (d_dt / (1.0 + jnp.exp(-raw))).astype(BF16)

    h_low, lam_low = carried(state_ref)
    g_scaled, x_weighted = [], []
    for j in range(FINISH_LANES // 256):
        copy = spread(step * (FINISH_LANES // DIM) + 4 * j, 256)
        lanes = slice(j * 256, (j + 1) * 256)
        start = dot(half_ref[1], copy)
        from_state = start * dot(c_ref[...], h_low[:, lanes])
        y_ref[:, lanes] = (ymix_ref[:, lanes].astype(F32) + from_state).astype(BF16)
        g_scaled.append((start * g_ref[:, lanes].astype(F32)).astype(BF16))
        weight = dot(half_ref[0], copy)
        from_grad = weight * dot(b_ref[...], lam_low[:, lanes])
        dx_ref[:, lanes] = (dxmix_ref[:, lanes].astype(F32) + from_grad).astype(BF16)
        x_weighted.append((weight * x_ref[:, lanes].astype(F32)).astype(BF16))
    dc_ref[...] += dot_nt(jnp.concatenate(g_scaled, axis=1), h_low)
    db_ref[...] += dot_nt(jnp.concatenate(x_weighted, axis=1), lam_low)


def finish(
    x, g, ymix, dxmix, state, b, c, half, dbmix, dcmix, raw_t, rate, scal, grads, ddt
):
    lanes = FINISH_LANES
    return pl.pallas_call(
        finish_kernel,
        grid=(WIDTH // lanes,),
        in_specs=[
            wide(lanes), wide(lanes), wide(lanes), wide(lanes), pieces(lanes, CARRY),
            whole(BLOCK, STATE), whole(BLOCK, STATE),
            whole(3, BLOCK, 2 * HEADS), whole(BLOCK, STATE), whole(BLOCK, STATE),
            whole(HEADS, BLOCK), whole(HEADS, 128), whole(4, HEADS, BLOCK),
            whole(2, HEADS, BLOCK), whole(HEADS, BLOCK),
        ],
        out_specs=[
            wide(lanes), wide(lanes), whole(BLOCK, STATE), whole(BLOCK, STATE),
            whole(HEADS, BLOCK),
        ],
        out_shape=[
            like((BLOCK, WIDTH), BF16), like((BLOCK, WIDTH), BF16),
            like((BLOCK, STATE)), like((BLOCK, STATE)), like((HEADS, BLOCK), BF16),
        ],
        compiler_params=params(),
        cost_estimate=cost(8 * 10**9, 16 * 10**6, 10**5),
        name="finish",
    )(x, g, ymix, dxmix, state, b, c, half, dbmix, dcmix, raw_t, rate, scal, grads, ddt)


def body(inputs, dt_raw, b_proj, c_proj, a_log, d_skip, seg_ids, cotangent):
    everyone = ("seq", "head")
    mine = lax.axis_index("head")
    place = mine.astype(jnp.int32).reshape(1)
    group = a_log.shape[0]
    gains = lax.all_gather(jnp.stack([a_log, d_skip]), "head", tiled=True)
    raw_t = dt_raw.T
    pay, scal, cum2, half, rate, seg, skip = states(
        place, raw_t, gains, seg_ids.reshape(-1, 128), inputs, cotangent, b_proj, c_proj
    )
    pay = lax.all_to_all(pay, everyone, 0, 0, tiled=True)
    ymix, dxmix, cpart, ddt, dbmix, dcmix, dskip = mix(
        inputs, cotangent, b_proj, c_proj, seg, skip, cum2, half
    )
    state = lax.all_to_all(scan(pay), everyone, 0, 0, tiled=True)
    grads, sums = gradient_sums(inputs, cotangent, state, b_proj, c_proj, scal, cpart, dskip)
    sums = lax.all_to_all(sums.reshape(PARTS, 1, 128), everyone, 0, 0, tiled=True)
    y, dx, db, dc, raw_grad = finish(
        inputs, cotangent, ymix, dxmix, state, b_proj, c_proj, half, dbmix, dcmix,
        raw_t, rate, scal, grads, ddt,
    )
    sums = jnp.sum(sums, axis=(0, 1))
    a_grad = lax.dynamic_slice(sums, (mine * group,), (group,))
    skip_grad = lax.dynamic_slice(sums, (HEADS + mine * group,), (group,))
    return (y, dx, raw_grad.T, db, dc, a_grad, skip_grad)


def solution(mesh):
    tokens = P(("seq", "head"), None)
    in_specs = (tokens, tokens, tokens, tokens, P("head"), P("head"), P("seq"), tokens)
    out_specs = (tokens, tokens, tokens, tokens, tokens, P("head"), P("head"))
    return jax.shard_map(body, mesh=mesh, in_specs=in_specs, out_specs=out_specs, check_vma=False)
```

```python
import jax
import jax.numpy as jnp
from jax import lax
from jax.experimental import pallas as pl
from jax.experimental.pallas import tpu as pltpu
from jax.sharding import PartitionSpec as P

HEADS = 64
DIM = 64
STATE = 128
BLOCK = 256
WIDTH = HEADS * DIM
PARTS = 128
PIECE = STATE * WIDTH // (PARTS * 128)
ROWS = STATE // PIECE
CARRY = 2 * PIECE
META = 8
LOG2E = 1.4426950408889634
F32 = jnp.float32
BF16 = jnp.bfloat16


def dot(a, b):
    return jnp.dot(a, b, preferred_element_type=F32)


def dot_nt(a, b):
    return lax.dot_general(a, b, (((1,), (1,)), ((), ())), preferred_element_type=F32)


def dot_tn(a, b):
    return lax.dot_general(a, b, (((0,), (0,)), ((), ())), preferred_element_type=F32)


def iota(shape, axis):
    return lax.broadcasted_iota(jnp.int32, shape, axis)


def ones_where(mask):
    return jnp.where(mask, 1.0, 0.0).astype(BF16)


def split2(value):
    high = value.astype(BF16)
    return high, (value - high.astype(F32)).astype(BF16)


def split3(value):
    high = value.astype(BF16)
    return (high,) + split2(value - high.astype(F32))


def spread(head0, lanes):
    shape = (2 * HEADS, lanes)
    return ones_where((iota(shape, 0) & (HEADS - 1)) == (iota(shape, 1) >> 6) + head0)


def gather_heads(head0, lanes, period):
    shape = (lanes, HEADS)
    return ones_where(((iota(shape, 0) & (period - 1)) >> 6) + head0 == iota(shape, 1))


def whole(*shape):
    return pl.BlockSpec(shape, lambda *_: (0,) * len(shape))


def wide(lanes):
    return pl.BlockSpec((BLOCK, lanes), lambda i: (0, i))


def moment(lanes):
    return pl.BlockSpec((STATE, lanes), lambda i: (0, i))


def pieces(lanes, rows):
    return pl.BlockSpec((PARTS * lanes // WIDTH, rows, 128), lambda i: (i, 0, 0))


def params(mib=62):
    return pltpu.CompilerParams(vmem_limit_bytes=mib * 1024 * 1024)


def cost(flops, moved, exps):
    return pl.CostEstimate(flops=flops, bytes_accessed=moved, transcendentals=exps)


def like(shape, kind=F32):
    return jax.ShapeDtypeStruct(shape, kind)


STATES_LANES = 2048


def heads_row(gains, row):
    return jnp.concatenate([gains[k : k + 1] for k in range(row, gains.shape[0], 2)], axis=1)


def states_kernel(
    place_ref, raw_ref, gains_ref, seg_ref, x_ref, g_ref, b_ref, c_ref,
    pay_ref, scal_ref, cum2_ref, half_ref, rate_ref, row_ref, skip_ref,
    bt_ref, ct_ref, meta_ref,
):
    step = pl.program_id(0)

    @pl.when(step == 0)
    def _():
        raw = raw_ref[...].astype(F32)
        dt = jnp.maximum(raw, 0.0) + jnp.log1p(jnp.exp(-jnp.abs(raw)))
        square = (BLOCK, BLOCK)
        upto = ones_where(iota(square, 0) <= iota(square, 1))
        high, mid, low = split3(dt)
        sums = dot(high, upto) + dot(mid, upto) + dot(low, upto)
        gains = gains_ref[...]
        alog = heads_row(gains, 0)
        skip = jnp.broadcast_to(heads_row(gains, 1), (16, HEADS))
        skip_ref[...] = jnp.concatenate(split2(skip), axis=1)
        rate = jnp.exp(jnp.broadcast_to(alog, (128, HEADS)).T)
        cum = -rate[:, :1] * sums
        tot = cum[:, BLOCK - 1 :]
        block = 2 * (place_ref[0] % (seg_ref.shape[0] // 2))
        seg = jnp.concatenate(
            [seg_ref[pl.ds(block, 1), :], seg_ref[pl.ds(block + 1, 1), :]], axis=1
        ).astype(F32)
        first, last = seg[:, :1], seg[:, BLOCK - 1 :]
        end = jnp.where(seg == last, jnp.exp(tot - cum), 0.0)
        start = jnp.where(seg == first, jnp.exp(cum), 0.0)
        weight = end * dt
        scal_ref[0] = end
        scal_ref[1] = weight
        scal_ref[2] = start
        scal_ref[3] = cum
        cum2_ref[...] = cum * LOG2E
        half_ref[0] = jnp.concatenate(split2(weight), axis=0).T
        half_ref[1] = jnp.concatenate(split2(start), axis=0).T
        half_ref[2] = jnp.concatenate(split2(dt), axis=0).T
        half_ref[3] = jnp.concatenate(split2(cum * start), axis=0).T
        half_ref[4] = jnp.concatenate(split2((tot - cum) * weight), axis=0).T
        rate_ref[...] = rate
        row_ref[...] = seg
        bt_ref[...] = b_ref[...].T
        ct_ref[...] = c_ref[...].T
        kind = iota((HEADS, 128), 1)
        columns = jnp.zeros((HEADS, 128), F32)
        for k, part in enumerate(split3(tot)):
            columns = jnp.where(kind == k, part.astype(F32), columns)
        columns = jnp.where(kind == 3, first, jnp.where(kind == 4, last, columns))
        rows = jnp.concatenate([columns, jnp.zeros((HEADS, 128), F32)], axis=0).T
        meta_ref[...] = rows[:16].astype(BF16)

    copy = spread(step * (STATES_LANES // DIM), STATES_LANES)
    meta = dot(meta_ref[...], copy)[:META].astype(BF16)
    x_weighted = (x_ref[...].astype(F32) * dot(half_ref[0], copy)).astype(BF16)
    contrib = dot(bt_ref[...], x_weighted).astype(BF16)
    g_scaled = (g_ref[...].astype(F32) * dot(half_ref[1], copy)).astype(BF16)
    dh_low = dot(ct_ref[...], g_scaled).astype(BF16)
    for j in range(STATES_LANES // 128):
        lanes = slice(j * 128, (j + 1) * 128)
        for r in range(ROWS):
            rows = slice(r * PIECE, (r + 1) * PIECE)
            pay_ref[j * ROWS + r, :PIECE, :] = contrib[rows, lanes]
            pay_ref[j * ROWS + r, PIECE:CARRY, :] = dh_low[rows, lanes]
            pay_ref[j * ROWS + r, CARRY:, :] = meta[:, lanes]


def states(place, raw_t, gains, seg_ids, x, g, b, c):
    return pl.pallas_call(
        states_kernel,
        grid=(WIDTH // STATES_LANES,),
        in_specs=[
            pl.BlockSpec(memory_space=pltpu.SMEM),
            whole(HEADS, BLOCK), whole(*gains.shape), whole(*seg_ids.shape),
            wide(STATES_LANES), wide(STATES_LANES), whole(BLOCK, STATE), whole(BLOCK, STATE),
        ],
        out_specs=[
            pieces(STATES_LANES, CARRY + META), whole(4, HEADS, BLOCK), whole(HEADS, BLOCK),
            whole(5, BLOCK, 2 * HEADS), whole(HEADS, 128), whole(1, BLOCK), whole(16, 2 * HEADS),
        ],
        out_shape=[
            like((PARTS, CARRY + META, 128), BF16), like((4, HEADS, BLOCK)), like((HEADS, BLOCK)),
            like((5, BLOCK, 2 * HEADS), BF16), like((HEADS, 128)), like((1, BLOCK)),
            like((16, 2 * HEADS), BF16),
        ],
        scratch_shapes=[
            pltpu.VMEM((STATE, BLOCK), BF16),
            pltpu.VMEM((STATE, BLOCK), BF16),
            pltpu.VMEM((16, 2 * HEADS), BF16),
        ],
        compiler_params=params(),
        cost_estimate=cost(10**9, 8 * 10**6, 10**5),
        name="states",
    )(place, raw_t, gains, seg_ids, x, g, b, c)


MIX_LANES = 1024
HALF = BLOCK // 2


def mix_kernel(
    x_ref, g_ref, b_ref, c_ref, seg_ref, skip_ref, cum2_ref, half_ref,
    y_ref, dx_ref, cpart_ref, ddt_ref, db_ref, dc_ref, dskip_ref, start_mom_ref, end_mom_ref,
    gram_ref, mask_ref, total_ref, cpart_sum_ref, ddt_sum_ref, dskip_sum_ref,
    bt_ref, ct_ref,
):
    step = pl.program_id(0)
    square = (BLOCK, BLOCK)

    @pl.when(step == 0)
    def _():
        seg_row = seg_ref[...]
        seg_col = jnp.broadcast_to(seg_row, square).T
        keep = (seg_row == seg_col) & (iota(square, 0) >= iota(square, 1))
        mask_ref[...] = jnp.where(keep, 0.0, -1e30)
        gram_ref[...] = dot_nt(c_ref[...], b_ref[...])
        total_ref[...] = jnp.zeros_like(total_ref)
        cpart_sum_ref[...] = jnp.zeros_like(cpart_sum_ref)
        ddt_sum_ref[...] = jnp.zeros_like(ddt_sum_ref)
        dskip_sum_ref[...] = jnp.zeros_like(dskip_sum_ref)
        bt_ref[...] = b_ref[...].T
        ct_ref[...] = c_ref[...].T

    copy = spread(step * (MIX_LANES // DIM), MIX_LANES)
    g_moment = (g_ref[...].astype(F32) * dot(half_ref[3], copy)).astype(BF16)
    start_mom_ref[...] = dot(ct_ref[...], g_moment).astype(BF16)
    x_moment = (x_ref[...].astype(F32) * dot(half_ref[4], copy)).astype(BF16)
    end_mom_ref[...] = dot(bt_ref[...], x_moment).astype(BF16)
    lower = iota((BLOCK, 128), 1) < DIM
    zero = jnp.zeros((BLOCK, 128), BF16)
    cum2 = cum2_ref[...]
    columns = cum2.T
    for j in range(MIX_LANES // 128):
        head0 = step * (MIX_LANES // DIM) + 2 * j
        lanes = slice(j * 128, (j + 1) * 128)
        x_low = x_ref[:, lanes]
        g_low = g_ref[:, lanes]
        x = x_low.astype(F32)
        g = g_low.astype(F32)
        copy = spread(head0, 128)
        dt = dot(half_ref[2], copy)
        x_dt = (x * dt).astype(BF16)
        ys = [jnp.zeros((HALF, 128), F32)] * 2
        dxs = [jnp.zeros((HALF, 128), F32), jnp.zeros((BLOCK, 128), F32)]
        for k in range(2):
            pick = lower if k == 0 else ~lower
            g_one = jnp.where(pick, g_low, zero)
            x_one = jnp.where(pick, x_dt, zero)
            head = 2 * j + k
            col, row = columns[:, head : head + 1], cum2[head : head + 1, :]
            for rows, upto in ((slice(0, HALF), HALF), (slice(HALF, BLOCK), BLOCK)):
                kern = jnp.exp2(col[rows] - row[:, :upto] + mask_ref[rows, :upto])
                mixed = (gram_ref[rows, :upto] * kern).astype(BF16)
                total_ref[rows, :upto] += dot_nt(g_one[rows], x_dt[:upto]) * kern
                ys[rows.start // HALF] += dot(mixed, x_one[:upto])
                dxs[rows.start // HALF] += dot_tn(mixed, g_one[rows])
        y = jnp.concatenate(ys, axis=0)
        dx = jnp.concatenate([dxs[0] + dxs[1][:HALF], dxs[1][HALF:]], axis=0)
        skip = dot(skip_ref[...], copy)[:1]
        gather = gather_heads(head0, 256, 128)
        y_ref[:, lanes] = (y + skip * x).astype(BF16)
        dx_ref[:, lanes] = (dx * dt + skip * g).astype(BF16)
        apart = jnp.concatenate(split2(g * y - x_dt.astype(F32) * dx), axis=1)
        cpart_sum_ref[...] += dot(apart, gather)
        ddt_sum_ref[...] += dot((x * dx).astype(BF16), gather[:128])
        channel_sum = jnp.broadcast_to(jnp.sum(g * x, axis=0, keepdims=True), (8, 128))
        dskip_sum_ref[...] += dot(jnp.concatenate(split2(channel_sum), axis=1), gather)

    @pl.when(step == WIDTH // MIX_LANES - 1)
    def _():
        total = total_ref[...].astype(BF16)
        dc_ref[...] = dot(total, b_ref[...])
        db_ref[...] = dot_tn(total, c_ref[...])
        cpart_ref[...] = cpart_sum_ref[...].T
        ddt_ref[...] = ddt_sum_ref[...].T
        dskip_ref[...] = jnp.broadcast_to(dskip_sum_ref[:1], (128, HEADS)).T


def mix(x, g, b, c, seg, skip, cum2, half):
    return pl.pallas_call(
        mix_kernel,
        grid=(WIDTH // MIX_LANES,),
        in_specs=[
            wide(MIX_LANES), wide(MIX_LANES), whole(BLOCK, STATE), whole(BLOCK, STATE),
            whole(1, BLOCK),
            whole(16, 2 * HEADS),
            pl.BlockSpec((MIX_LANES // DIM, BLOCK), lambda i: (i, 0)),
            whole(5, BLOCK, 2 * HEADS),
        ],
        out_specs=[
            wide(MIX_LANES), wide(MIX_LANES), whole(HEADS, BLOCK), whole(HEADS, BLOCK),
            whole(BLOCK, STATE), whole(BLOCK, STATE), whole(HEADS, 128),
            moment(MIX_LANES), moment(MIX_LANES),
        ],
        out_shape=[
            like((BLOCK, WIDTH), BF16), like((BLOCK, WIDTH), BF16),
            like((HEADS, BLOCK)), like((HEADS, BLOCK)),
            like((BLOCK, STATE)), like((BLOCK, STATE)), like((HEADS, 128)),
            like((STATE, WIDTH), BF16), like((STATE, WIDTH), BF16),
        ],
        scratch_shapes=[pltpu.VMEM((BLOCK, BLOCK), F32)] * 3
        + [pltpu.VMEM((BLOCK, HEADS), F32)] * 2
        + [pltpu.VMEM((8, HEADS), F32)]
        + [pltpu.VMEM((STATE, BLOCK), BF16)] * 2,
        compiler_params=params(),
        cost_estimate=cost(20 * 10**9, 9 * 10**6, 4 * 10**6),
        name="mix",
    )(x, g, b, c, seg, skip, cum2, half)


def scan_kernel(pay_ref, out_ref):
    square = (PARTS, PARTS)
    notes = jnp.swapaxes(pay_ref[:, CARRY:, :].astype(F32), 0, 1)
    high, mid, low, first, last = (notes[k] for k in range(5))
    upto = ones_where(iota(square, 0) >= iota(square, 1))
    through = dot(upto, high.astype(BF16)) + dot(upto, mid.astype(BF16)) + dot(upto, low.astype(BF16))
    ahead = through - (high + mid + low)
    through_t = through.T
    keep = (iota(square, 0) > iota(square, 1)) & (first[:, :1] == last.T[:1, :])
    forward, backward = [], []
    for lane in (0, DIM):
        gap = ahead[:, lane : lane + 1] - through_t[lane : lane + 1, :]
        carry = jnp.where(keep, jnp.exp(jnp.minimum(gap, 0.0)), 0.0)
        forward.append(carry.astype(BF16))
        backward.append(carry.T.astype(BF16))
    forward = jnp.concatenate(forward, axis=0)
    backward = jnp.concatenate(backward, axis=0)
    lower = iota((PARTS, 256), 1) & (128 - 1) < DIM

    for k in range(0, CARRY, 16):
        block = jnp.swapaxes(pay_ref[:, k : k + 16, :], 0, 1)
        done = []
        for i in range(0, 16, 2):
            rows = jnp.concatenate([block[i], block[i + 1]], axis=1)
            both = dot(forward if k < PIECE else backward, rows)
            pair = jnp.where(lower, both[:PARTS], both[PARTS:]).astype(BF16)
            done += [pair[:, :128], pair[:, 128:]]
        out_ref[:, k : k + 16, :] = jnp.swapaxes(jnp.stack(done), 0, 1)


def scan(pay):
    return pl.pallas_call(
        scan_kernel,
        out_shape=like((PARTS, CARRY, 128), BF16),
        in_specs=[pl.BlockSpec(memory_space=pltpu.VMEM)],
        out_specs=pl.BlockSpec(memory_space=pltpu.VMEM),
        compiler_params=params(16),
        cost_estimate=cost(5 * 10**8, 5 * 10**6, 10**5),
        name="scan",
    )(pay)


def carried(state_ref):
    tiles = [state_ref[k : k + ROWS] for k in range(0, state_ref.shape[0], ROWS)]
    h_low = jnp.concatenate([tile[:, :PIECE].reshape(STATE, 128) for tile in tiles], axis=1)
    lam_low = jnp.concatenate([tile[:, PIECE:].reshape(STATE, 128) for tile in tiles], axis=1)
    return h_low, lam_low


SUMS_LANES = 2048


def sums_kernel(
    start_mom_ref, end_mom_ref, state_ref, scal_ref, cpart_ref, dskip_ref,
    ddecay_ref, sums_ref,
    total_ref,
):
    step = pl.program_id(0)

    @pl.when(step == 0)
    def _():
        total_ref[...] = jnp.zeros_like(total_ref)

    h_low, lam_low = carried(state_ref)
    h = h_low.astype(F32)
    lam = lam_low.astype(F32)
    moments = h * start_mom_ref[...].astype(F32) + lam * end_mom_ref[...].astype(F32)
    moments = jnp.sum(moments, axis=0, keepdims=True)
    inner = jnp.sum(h * lam, axis=0, keepdims=True)
    kind = iota((16, SUMS_LANES), 0)
    rows = jnp.where(kind == 0, moments, jnp.where(kind == 1, inner, 0.0))
    gather = gather_heads(step * (SUMS_LANES // DIM), SUMS_LANES, SUMS_LANES)
    high, low = split2(rows)
    total_ref[...] += dot(high, gather) + dot(low, gather)

    @pl.when(step == WIDTH // SUMS_LANES - 1)
    def _():
        total = jnp.concatenate(
            [total_ref[...], jnp.zeros((128 - 16, HEADS), F32)], axis=0
        ).T
        d_decay = total[:, 1:2]
        start, cum = scal_ref[2], scal_ref[3]
        at_end = cum[:, BLOCK - 1 :] * start[:, BLOCK - 1 :]
        inside = jnp.sum(cum * cpart_ref[...], axis=1, keepdims=True)
        rate_grad = inside + total[:, :1] + at_end * d_decay
        ddecay_ref[...] = jnp.broadcast_to(d_decay, (HEADS, 128))
        column = jnp.concatenate([rate_grad, dskip_ref[:, :1]], axis=0)
        sums_ref[...] = jnp.broadcast_to(column, (PARTS, 128)).T


def gradient_sums(start_mom, end_mom, state, scal, cpart, dskip):
    return pl.pallas_call(
        sums_kernel,
        grid=(WIDTH // SUMS_LANES,),
        in_specs=[
            moment(SUMS_LANES), moment(SUMS_LANES), pieces(SUMS_LANES, CARRY),
            whole(4, HEADS, BLOCK), whole(HEADS, BLOCK), whole(HEADS, 128),
        ],
        out_specs=[whole(HEADS, 128), whole(PARTS, 128)],
        out_shape=[like((HEADS, 128)), like((PARTS, 128))],
        scratch_shapes=[pltpu.VMEM((16, HEADS), F32)],
        compiler_params=params(),
        cost_estimate=cost(10**8, 4 * 10**6, 10**4),
        name="gradient_sums",
    )(start_mom, end_mom, state, scal, cpart, dskip)


FINISH_LANES = 1024


def finish_kernel(
    x_ref, g_ref, ymix_ref, dxmix_ref, state_ref, b_ref, c_ref, half_ref, dbmix_ref, dcmix_ref,
    raw_ref, rate_ref, scal_ref, cpart_ref, ddecay_ref, ddt_ref,
    y_ref, dx_ref, db_ref, dc_ref, raw_grad_ref,
    dstart_ref, dweight_ref,
):
    step = pl.program_id(0)

    @pl.when(step == 0)
    def _():
        db_ref[...] = dbmix_ref[...]
        dc_ref[...] = dcmix_ref[...]
        dstart_ref[...] = jnp.zeros_like(dstart_ref)
        dweight_ref[...] = jnp.zeros_like(dweight_ref)

    h_low, lam_low = carried(state_ref)
    g_scaled, x_weighted, start_terms, weight_terms = [], [], [], []
    for j in range(FINISH_LANES // 256):
        copy = spread(step * (FINISH_LANES // DIM) + 4 * j, 256)
        lanes = slice(j * 256, (j + 1) * 256)
        start = dot(half_ref[1], copy)
        g = g_ref[:, lanes].astype(F32)
        from_state = start * dot(c_ref[...], h_low[:, lanes])
        start_terms.append((g * from_state).astype(BF16))
        y_ref[:, lanes] = (ymix_ref[:, lanes].astype(F32) + from_state).astype(BF16)
        g_scaled.append((start * g).astype(BF16))
        weight = dot(half_ref[0], copy)
        x = x_ref[:, lanes].astype(F32)
        plain_grad = dot(b_ref[...], lam_low[:, lanes])
        weight_terms.append((x * plain_grad).astype(BF16))
        from_grad = weight * plain_grad
        dx_ref[:, lanes] = (dxmix_ref[:, lanes].astype(F32) + from_grad).astype(BF16)
        x_weighted.append((weight * x).astype(BF16))
    dc_ref[...] += dot_nt(jnp.concatenate(g_scaled, axis=1), h_low)
    db_ref[...] += dot_nt(jnp.concatenate(x_weighted, axis=1), lam_low)
    gather = gather_heads(step * (FINISH_LANES // DIM), FINISH_LANES, FINISH_LANES)
    dstart_ref[...] += dot(jnp.concatenate(start_terms, axis=1), gather)
    dweight_ref[...] += dot(jnp.concatenate(weight_terms, axis=1), gather)

    @pl.when(step == WIDTH // FINISH_LANES - 1)
    def _():
        end, weight, start = (scal_ref[k] for k in range(3))
        d_weight = dweight_ref[...].T
        used = d_weight * weight
        d_cum = cpart_ref[...] + dstart_ref[...].T - used
        at_last = iota((HEADS, BLOCK), 1) == BLOCK - 1
        d_total = jnp.sum(used, axis=1, keepdims=True)
        d_total = d_total + ddecay_ref[:, :1] * start[:, BLOCK - 1 :]
        d_cum = d_cum + jnp.where(at_last, d_total, 0.0)
        square = (BLOCK, BLOCK)
        onward = ones_where(iota(square, 0) >= iota(square, 1))
        high, mid, low = split3(d_cum)
        d_log = dot(high, onward) + dot(mid, onward) + dot(low, onward)
        d_dt = ddt_ref[...] + d_weight * end - rate_ref[:, :1] * d_log
        raw = raw_ref[...].astype(F32)
        raw_grad_ref[...] = (d_dt / (1.0 + jnp.exp(-raw))).astype(BF16)


def finish(
    x, g, ymix, dxmix, state, b, c, half, dbmix, dcmix, raw_t, rate, scal, cpart, ddecay, ddt
):
    lanes = FINISH_LANES
    return pl.pallas_call(
        finish_kernel,
        grid=(WIDTH // lanes,),
        in_specs=[
            wide(lanes), wide(lanes), wide(lanes), wide(lanes), pieces(lanes, CARRY),
            whole(BLOCK, STATE), whole(BLOCK, STATE),
            whole(5, BLOCK, 2 * HEADS), whole(BLOCK, STATE), whole(BLOCK, STATE),
            whole(HEADS, BLOCK), whole(HEADS, 128), whole(4, HEADS, BLOCK),
            whole(HEADS, BLOCK), whole(HEADS, 128), whole(HEADS, BLOCK),
        ],
        out_specs=[
            wide(lanes), wide(lanes), whole(BLOCK, STATE), whole(BLOCK, STATE),
            whole(HEADS, BLOCK),
        ],
        out_shape=[
            like((BLOCK, WIDTH), BF16), like((BLOCK, WIDTH), BF16),
            like((BLOCK, STATE)), like((BLOCK, STATE)), like((HEADS, BLOCK), BF16),
        ],
        scratch_shapes=[pltpu.VMEM((BLOCK, HEADS), F32)] * 2,
        compiler_params=params(),
        cost_estimate=cost(8 * 10**9, 16 * 10**6, 10**5),
        name="finish",
    )(x, g, ymix, dxmix, state, b, c, half, dbmix, dcmix, raw_t, rate, scal, cpart, ddecay, ddt)


def body(inputs, dt_raw, b_proj, c_proj, a_log, d_skip, seg_ids, cotangent):
    everyone = ("seq", "head")
    mine = lax.axis_index("head")
    place = mine.astype(jnp.int32).reshape(1)
    group = a_log.shape[0]
    gains = lax.all_gather(jnp.stack([a_log, d_skip]), "head", tiled=True)
    raw_t = dt_raw.T
    pay, scal, cum2, half, rate, seg, skip = states(
        place, raw_t, gains, seg_ids.reshape(-1, 128), inputs, cotangent, b_proj, c_proj
    )
    pay = lax.all_to_all(pay, everyone, 0, 0, tiled=True)
    ymix, dxmix, cpart, ddt, dbmix, dcmix, dskip, start_mom, end_mom = mix(
        inputs, cotangent, b_proj, c_proj, seg, skip, cum2, half
    )
    state = lax.all_to_all(scan(pay), everyone, 0, 0, tiled=True)
    ddecay, sums = gradient_sums(start_mom, end_mom, state, scal, cpart, dskip)
    sums = lax.all_to_all(sums.reshape(PARTS, 1, 128), everyone, 0, 0, tiled=True)
    y, dx, db, dc, raw_grad = finish(
        inputs, cotangent, ymix, dxmix, state, b_proj, c_proj, half, dbmix, dcmix,
        raw_t, rate, scal, cpart, ddecay, ddt,
    )
    sums = jnp.sum(sums, axis=(0, 1))
    a_grad = lax.dynamic_slice(sums, (mine * group,), (group,))
    skip_grad = lax.dynamic_slice(sums, (HEADS + mine * group,), (group,))
    return (y, dx, raw_grad.T, db, dc, a_grad, skip_grad)


def solution(mesh):
    tokens = P(("seq", "head"), None)
    in_specs = (tokens, tokens, tokens, tokens, P("head"), P("head"), P("seq"), tokens)
    out_specs = (tokens, tokens, tokens, tokens, tokens, P("head"), P("head"))
    return jax.shard_map(body, mesh=mesh, in_specs=in_specs, out_specs=out_specs, check_vma=False)
```

```python
import jax
import jax.numpy as jnp
from jax import lax
from jax.experimental import pallas as pl
from jax.experimental.pallas import tpu as pltpu
from jax.sharding import PartitionSpec as P

HEADS = 64
DIM = 64
STATE = 128
BLOCK = 256
WIDTH = HEADS * DIM
PARTS = 128
PIECE = STATE * WIDTH // (PARTS * 128)
ROWS = STATE // PIECE
CARRY = 2 * PIECE
META = 8
LOG2E = 1.4426950408889634
F32 = jnp.float32
BF16 = jnp.bfloat16


def dot(a, b):
    return jnp.dot(a, b, preferred_element_type=F32)


def dot_nt(a, b):
    return lax.dot_general(a, b, (((1,), (1,)), ((), ())), preferred_element_type=F32)


def dot_tn(a, b):
    return lax.dot_general(a, b, (((0,), (0,)), ((), ())), preferred_element_type=F32)


def iota(shape, axis):
    return lax.broadcasted_iota(jnp.int32, shape, axis)


def ones_where(mask):
    return jnp.where(mask, 1.0, 0.0).astype(BF16)


def split2(value):
    high = value.astype(BF16)
    return high, (value - high.astype(F32)).astype(BF16)


def split3(value):
    high = value.astype(BF16)
    return (high,) + split2(value - high.astype(F32))


def spread(head0, lanes):
    shape = (2 * HEADS, lanes)
    return ones_where((iota(shape, 0) & (HEADS - 1)) == (iota(shape, 1) >> 6) + head0)


def gather_heads(head0, lanes, period):
    shape = (lanes, HEADS)
    return ones_where(((iota(shape, 0) & (period - 1)) >> 6) + head0 == iota(shape, 1))


def whole(*shape):
    return pl.BlockSpec(shape, lambda *_: (0,) * len(shape))


def wide(lanes):
    return pl.BlockSpec((BLOCK, lanes), lambda i: (0, i))


def moment(lanes):
    return pl.BlockSpec((STATE, lanes), lambda i: (0, i))


def pieces(lanes, rows):
    return pl.BlockSpec((PARTS * lanes // WIDTH, rows, 128), lambda i: (i, 0, 0))


def params(mib=62):
    return pltpu.CompilerParams(vmem_limit_bytes=mib * 1024 * 1024)


def cost(flops, moved, exps):
    return pl.CostEstimate(flops=flops, bytes_accessed=moved, transcendentals=exps)


def like(shape, kind=F32):
    return jax.ShapeDtypeStruct(shape, kind)


STATES_LANES = 2048


def heads_row(gains, row):
    return jnp.concatenate([gains[k : k + 1] for k in range(row, gains.shape[0], 2)], axis=1)


def states_kernel(
    place_ref, raw_ref, gains_ref, seg_ref, x_ref, g_ref, b_ref, c_ref,
    pay_ref, scal_ref, cum2_ref, half_ref, rate_ref, row_ref, skip_ref,
    bt_ref, ct_ref, meta_ref,
):
    step = pl.program_id(0)

    @pl.when(step == 0)
    def _():
        raw = raw_ref[...].astype(F32)
        dt = jnp.maximum(raw, 0.0) + jnp.log1p(jnp.exp(-jnp.abs(raw)))
        square = (BLOCK, BLOCK)
        upto = ones_where(iota(square, 0) <= iota(square, 1))
        high, mid, low = split3(dt)
        sums = dot(high, upto) + dot(mid, upto) + dot(low, upto)
        gains = gains_ref[...]
        alog = heads_row(gains, 0)
        skip = jnp.broadcast_to(heads_row(gains, 1), (16, HEADS))
        skip_ref[...] = jnp.concatenate(split2(skip), axis=1)
        rate = jnp.exp(jnp.broadcast_to(alog, (128, HEADS)).T)
        cum = -rate[:, :1] * sums
        tot = cum[:, BLOCK - 1 :]
        block = 2 * (place_ref[0] % (seg_ref.shape[0] // 2))
        seg = jnp.concatenate(
            [seg_ref[pl.ds(block, 1), :], seg_ref[pl.ds(block + 1, 1), :]], axis=1
        ).astype(F32)
        first, last = seg[:, :1], seg[:, BLOCK - 1 :]
        end = jnp.where(seg == last, jnp.exp(tot - cum), 0.0)
        start = jnp.where(seg == first, jnp.exp(cum), 0.0)
        weight = end * dt
        scal_ref[0] = end
        scal_ref[1] = weight
        scal_ref[2] = start
        scal_ref[3] = cum
        cum2_ref[...] = cum * LOG2E
        half_ref[0] = jnp.concatenate(split2(weight), axis=0).T
        half_ref[1] = jnp.concatenate(split2(start), axis=0).T
        half_ref[2] = jnp.concatenate(split2(dt), axis=0).T
        half_ref[3] = jnp.concatenate(split2(cum * start), axis=0).T
        half_ref[4] = jnp.concatenate(split2((tot - cum) * weight), axis=0).T
        rate_ref[...] = rate
        row_ref[...] = seg
        bt_ref[...] = b_ref[...].T
        ct_ref[...] = c_ref[...].T
        kind = iota((HEADS, 128), 1)
        columns = jnp.zeros((HEADS, 128), F32)
        for k, part in enumerate(split3(tot)):
            columns = jnp.where(kind == k, part.astype(F32), columns)
        columns = jnp.where(kind == 3, first, jnp.where(kind == 4, last, columns))
        rows = jnp.concatenate([columns, jnp.zeros((HEADS, 128), F32)], axis=0).T
        meta_ref[...] = rows[:16].astype(BF16)

    copy = spread(step * (STATES_LANES // DIM), STATES_LANES)
    meta = dot(meta_ref[...], copy)[:META].astype(BF16)
    x_weighted = (x_ref[...].astype(F32) * dot(half_ref[0], copy)).astype(BF16)
    contrib = dot(bt_ref[...], x_weighted).astype(BF16)
    g_scaled = (g_ref[...].astype(F32) * dot(half_ref[1], copy)).astype(BF16)
    dh_low = dot(ct_ref[...], g_scaled).astype(BF16)
    for j in range(STATES_LANES // 128):
        lanes = slice(j * 128, (j + 1) * 128)
        for r in range(ROWS):
            rows = slice(r * PIECE, (r + 1) * PIECE)
            pay_ref[j * ROWS + r, :PIECE, :] = contrib[rows, lanes]
            pay_ref[j * ROWS + r, PIECE:CARRY, :] = dh_low[rows, lanes]
            pay_ref[j * ROWS + r, CARRY:, :] = meta[:, lanes]


def states(place, raw_t, gains, seg_ids, x, g, b, c):
    return pl.pallas_call(
        states_kernel,
        grid=(WIDTH // STATES_LANES,),
        in_specs=[
            pl.BlockSpec(memory_space=pltpu.SMEM),
            whole(HEADS, BLOCK), whole(*gains.shape), whole(*seg_ids.shape),
            wide(STATES_LANES), wide(STATES_LANES), whole(BLOCK, STATE), whole(BLOCK, STATE),
        ],
        out_specs=[
            pieces(STATES_LANES, CARRY + META), whole(4, HEADS, BLOCK), whole(HEADS, BLOCK),
            whole(5, BLOCK, 2 * HEADS), whole(HEADS, 128), whole(1, BLOCK), whole(16, 2 * HEADS),
        ],
        out_shape=[
            like((PARTS, CARRY + META, 128), BF16), like((4, HEADS, BLOCK)), like((HEADS, BLOCK)),
            like((5, BLOCK, 2 * HEADS), BF16), like((HEADS, 128)), like((1, BLOCK)),
            like((16, 2 * HEADS), BF16),
        ],
        scratch_shapes=[
            pltpu.VMEM((STATE, BLOCK), BF16),
            pltpu.VMEM((STATE, BLOCK), BF16),
            pltpu.VMEM((16, 2 * HEADS), BF16),
        ],
        compiler_params=params(),
        cost_estimate=cost(10**9, 8 * 10**6, 10**5),
        name="states",
    )(place, raw_t, gains, seg_ids, x, g, b, c)


MIX_LANES = 1024
HALF = BLOCK // 2


def mix_kernel(
    x_ref, g_ref, b_ref, c_ref, seg_ref, skip_ref, cum2_ref, half_ref,
    y_ref, dx_ref, cpart_ref, ddt_ref, db_ref, dc_ref, dskip_ref, start_mom_ref, end_mom_ref,
    gram_ref, mask_ref, total_ref, cpart_sum_ref, ddt_sum_ref, dskip_sum_ref,
    bt_ref, ct_ref,
):
    step = pl.program_id(0)
    square = (BLOCK, BLOCK)

    @pl.when(step == 0)
    def _():
        seg_row = seg_ref[...]
        seg_col = jnp.broadcast_to(seg_row, square).T
        keep = (seg_row == seg_col) & (iota(square, 0) >= iota(square, 1))
        mask_ref[...] = jnp.where(keep, 0.0, -1e30)
        gram_ref[...] = dot_nt(c_ref[...], b_ref[...])
        total_ref[...] = jnp.zeros_like(total_ref)
        cpart_sum_ref[...] = jnp.zeros_like(cpart_sum_ref)
        ddt_sum_ref[...] = jnp.zeros_like(ddt_sum_ref)
        dskip_sum_ref[...] = jnp.zeros_like(dskip_sum_ref)
        bt_ref[...] = b_ref[...].T
        ct_ref[...] = c_ref[...].T

    copy = spread(step * (MIX_LANES // DIM), MIX_LANES)
    g_moment = (g_ref[...].astype(F32) * dot(half_ref[3], copy)).astype(BF16)
    start_mom_ref[...] = dot(ct_ref[...], g_moment).astype(BF16)
    x_moment = (x_ref[...].astype(F32) * dot(half_ref[4], copy)).astype(BF16)
    end_mom_ref[...] = dot(bt_ref[...], x_moment).astype(BF16)
    lower = iota((BLOCK, 128), 1) < DIM
    zero = jnp.zeros((BLOCK, 128), BF16)
    cum2 = cum2_ref[...]
    columns = cum2.T
    for j in range(MIX_LANES // 128):
        head0 = step * (MIX_LANES // DIM) + 2 * j
        lanes = slice(j * 128, (j + 1) * 128)
        x_low = x_ref[:, lanes]
        g_low = g_ref[:, lanes]
        x = x_low.astype(F32)
        g = g_low.astype(F32)
        copy = spread(head0, 128)
        dt = dot(half_ref[2], copy)
        x_dt = (x * dt).astype(BF16)
        ys = [jnp.zeros((HALF, 128), F32)] * 2
        dxs = [jnp.zeros((HALF, 128), F32), jnp.zeros((BLOCK, 128), F32)]
        for k in range(2):
            pick = lower if k == 0 else ~lower
            g_one = jnp.where(pick, g_low, zero)
            x_one = jnp.where(pick, x_dt, zero)
            head = 2 * j + k
            col, row = columns[:, head : head + 1], cum2[head : head + 1, :]
            for rows, upto in ((slice(0, HALF), HALF), (slice(HALF, BLOCK), BLOCK)):
                kern = jnp.exp2(col[rows] - row[:, :upto] + mask_ref[rows, :upto])
                mixed = (gram_ref[rows, :upto] * kern).astype(BF16)
                total_ref[rows, :upto] += dot_nt(g_one[rows], x_dt[:upto]) * kern
                ys[rows.start // HALF] += dot(mixed, x_one[:upto])
                dxs[rows.start // HALF] += dot_tn(mixed, g_one[rows])
        y = jnp.concatenate(ys, axis=0)
        dx = jnp.concatenate([dxs[0] + dxs[1][:HALF], dxs[1][HALF:]], axis=0)
        skip = dot(skip_ref[...], copy)[:1]
        gather = gather_heads(head0, 256, 128)
        y_ref[:, lanes] = (y + skip * x).astype(BF16)
        dx_ref[:, lanes] = (dx * dt + skip * g).astype(BF16)
        apart = jnp.concatenate(split2(g * y - x_dt.astype(F32) * dx), axis=1)
        cpart_sum_ref[...] += dot(apart, gather)
        ddt_sum_ref[...] += dot((x * dx).astype(BF16), gather[:128])
        channel_sum = jnp.broadcast_to(jnp.sum(g * x, axis=0, keepdims=True), (8, 128))
        dskip_sum_ref[...] += dot(jnp.concatenate(split2(channel_sum), axis=1), gather)

    @pl.when(step == WIDTH // MIX_LANES - 1)
    def _():
        total = total_ref[...].astype(BF16)
        dc_ref[...] = dot(total, b_ref[...])
        db_ref[...] = dot_tn(total, c_ref[...])
        cpart_ref[...] = cpart_sum_ref[...].T
        ddt_ref[...] = ddt_sum_ref[...].T
        dskip_ref[...] = jnp.broadcast_to(dskip_sum_ref[:1], (128, HEADS)).T


def mix(x, g, b, c, seg, skip, cum2, half):
    return pl.pallas_call(
        mix_kernel,
        grid=(WIDTH // MIX_LANES,),
        in_specs=[
            wide(MIX_LANES), wide(MIX_LANES), whole(BLOCK, STATE), whole(BLOCK, STATE),
            whole(1, BLOCK),
            whole(16, 2 * HEADS),
            pl.BlockSpec((MIX_LANES // DIM, BLOCK), lambda i: (i, 0)),
            whole(5, BLOCK, 2 * HEADS),
        ],
        out_specs=[
            wide(MIX_LANES), wide(MIX_LANES), whole(HEADS, BLOCK), whole(HEADS, BLOCK),
            whole(BLOCK, STATE), whole(BLOCK, STATE), whole(HEADS, 128),
            moment(MIX_LANES), moment(MIX_LANES),
        ],
        out_shape=[
            like((BLOCK, WIDTH), BF16), like((BLOCK, WIDTH), BF16),
            like((HEADS, BLOCK)), like((HEADS, BLOCK)),
            like((BLOCK, STATE)), like((BLOCK, STATE)), like((HEADS, 128)),
            like((STATE, WIDTH), BF16), like((STATE, WIDTH), BF16),
        ],
        scratch_shapes=[pltpu.VMEM((BLOCK, BLOCK), F32)] * 3
        + [pltpu.VMEM((BLOCK, HEADS), F32)] * 2
        + [pltpu.VMEM((8, HEADS), F32)]
        + [pltpu.VMEM((STATE, BLOCK), BF16)] * 2,
        compiler_params=params(),
        cost_estimate=cost(20 * 10**9, 9 * 10**6, 4 * 10**6),
        name="mix",
    )(x, g, b, c, seg, skip, cum2, half)


def scan_kernel(pay_ref, out_ref, matrix_ref):
    step = pl.program_id(0)

    @pl.when(step == 0)
    def _():
        prepare(pay_ref, matrix_ref)

    lower = iota((PARTS, 256), 1) & (128 - 1) < DIM
    first = step * 16
    matrix = matrix_ref[first // PIECE]
    for k in range(0, 16, 16):
        block = jnp.swapaxes(pay_ref[:, pl.ds(pl.multiple_of(first + k, 16), 16), :], 0, 1)
        done = []
        for i in range(0, 16, 2):
            rows = jnp.concatenate([block[i], block[i + 1]], axis=1)
            both = dot(matrix, rows)
            pair = jnp.where(lower, both[:PARTS], both[PARTS:]).astype(BF16)
            done += [pair[:, :128], pair[:, 128:]]
        out_ref[:, k : k + 16, :] = jnp.swapaxes(jnp.stack(done), 0, 1)


def prepare(pay_ref, matrix_ref):
    square = (PARTS, PARTS)
    notes = jnp.swapaxes(pay_ref[:, CARRY:, :].astype(F32), 0, 1)
    high, mid, low, first, last = (notes[k] for k in range(5))
    upto = ones_where(iota(square, 0) >= iota(square, 1))
    through = dot(upto, high.astype(BF16)) + dot(upto, mid.astype(BF16)) + dot(upto, low.astype(BF16))
    ahead = through - (high + mid + low)
    through_t = through.T
    keep = (iota(square, 0) > iota(square, 1)) & (first[:, :1] == last.T[:1, :])
    forward, backward = [], []
    for lane in (0, DIM):
        gap = ahead[:, lane : lane + 1] - through_t[lane : lane + 1, :]
        carry = jnp.where(keep, jnp.exp(jnp.minimum(gap, 0.0)), 0.0)
        forward.append(carry.astype(BF16))
        backward.append(carry.T.astype(BF16))
    forward = jnp.concatenate(forward, axis=0)
    backward = jnp.concatenate(backward, axis=0)
    matrix_ref[0] = forward
    matrix_ref[1] = backward


def scan(pay):
    return pl.pallas_call(
        scan_kernel,
        out_shape=like((PARTS, CARRY, 128), BF16),
        grid=(4,),
        in_specs=[whole(PARTS, CARRY + META, 128)],
        out_specs=pl.BlockSpec((PARTS, CARRY // 4, 128), lambda i: (0, i, 0)),
        scratch_shapes=[pltpu.VMEM((2, 2 * PARTS, PARTS), BF16)],
        compiler_params=params(16),
        cost_estimate=cost(5 * 10**8, 5 * 10**6, 10**5),
        name="scan",
    )(pay)


def carried(state_ref):
    tiles = [state_ref[k : k + ROWS] for k in range(0, state_ref.shape[0], ROWS)]
    h_low = jnp.concatenate([tile[:, :PIECE].reshape(STATE, 128) for tile in tiles], axis=1)
    lam_low = jnp.concatenate([tile[:, PIECE:].reshape(STATE, 128) for tile in tiles], axis=1)
    return h_low, lam_low


SUMS_LANES = 2048


def sums_kernel(
    start_mom_ref, end_mom_ref, state_ref, scal_ref, cpart_ref, dskip_ref,
    ddecay_ref, sums_ref,
    total_ref,
):
    step = pl.program_id(0)

    @pl.when(step == 0)
    def _():
        total_ref[...] = jnp.zeros_like(total_ref)

    h_low, lam_low = carried(state_ref)
    h = h_low.astype(F32)
    lam = lam_low.astype(F32)
    moments = h * start_mom_ref[...].astype(F32) + lam * end_mom_ref[...].astype(F32)
    moments = jnp.sum(moments, axis=0, keepdims=True)
    inner = jnp.sum(h * lam, axis=0, keepdims=True)
    kind = iota((16, SUMS_LANES), 0)
    rows = jnp.where(kind == 0, moments, jnp.where(kind == 1, inner, 0.0))
    gather = gather_heads(step * (SUMS_LANES // DIM), SUMS_LANES, SUMS_LANES)
    high, low = split2(rows)
    total_ref[...] += dot(high, gather) + dot(low, gather)

    @pl.when(step == WIDTH // SUMS_LANES - 1)
    def _():
        total = jnp.concatenate(
            [total_ref[...], jnp.zeros((128 - 16, HEADS), F32)], axis=0
        ).T
        d_decay = total[:, 1:2]
        start, cum = scal_ref[2], scal_ref[3]
        at_end = cum[:, BLOCK - 1 :] * start[:, BLOCK - 1 :]
        inside = jnp.sum(cum * cpart_ref[...], axis=1, keepdims=True)
        rate_grad = inside + total[:, :1] + at_end * d_decay
        ddecay_ref[...] = jnp.broadcast_to(d_decay, (HEADS, 128))
        column = jnp.concatenate([rate_grad, dskip_ref[:, :1]], axis=0)
        sums_ref[...] = jnp.broadcast_to(column, (PARTS, 128)).T


def gradient_sums(start_mom, end_mom, state, scal, cpart, dskip):
    return pl.pallas_call(
        sums_kernel,
        grid=(WIDTH // SUMS_LANES,),
        in_specs=[
            moment(SUMS_LANES), moment(SUMS_LANES), pieces(SUMS_LANES, CARRY),
            whole(4, HEADS, BLOCK), whole(HEADS, BLOCK), whole(HEADS, 128),
        ],
        out_specs=[whole(HEADS, 128), whole(PARTS, 128)],
        out_shape=[like((HEADS, 128)), like((PARTS, 128))],
        scratch_shapes=[pltpu.VMEM((16, HEADS), F32)],
        compiler_params=params(),
        cost_estimate=cost(10**8, 4 * 10**6, 10**4),
        name="gradient_sums",
    )(start_mom, end_mom, state, scal, cpart, dskip)


FINISH_LANES = 1024


def finish_kernel(
    x_ref, g_ref, ymix_ref, dxmix_ref, state_ref, b_ref, c_ref, half_ref, dbmix_ref, dcmix_ref,
    raw_ref, rate_ref, scal_ref, cpart_ref, ddecay_ref, ddt_ref,
    y_ref, dx_ref, db_ref, dc_ref, raw_grad_ref,
    terms_ref,
):
    step = pl.program_id(0)

    @pl.when(step == 0)
    def _():
        db_ref[...] = dbmix_ref[...]
        dc_ref[...] = dcmix_ref[...]
        terms_ref[...] = jnp.zeros_like(terms_ref)

    h_low, lam_low = carried(state_ref)
    g_scaled, x_weighted, start_terms, weight_terms = [], [], [], []
    for j in range(FINISH_LANES // 256):
        copy = spread(step * (FINISH_LANES // DIM) + 4 * j, 256)
        lanes = slice(j * 256, (j + 1) * 256)
        start = dot(half_ref[1], copy)
        g = g_ref[:, lanes].astype(F32)
        from_state = start * dot(c_ref[...], h_low[:, lanes])
        start_terms.append((g * from_state).astype(BF16))
        y_ref[:, lanes] = (ymix_ref[:, lanes].astype(F32) + from_state).astype(BF16)
        g_scaled.append((start * g).astype(BF16))
        weight = dot(half_ref[0], copy)
        x = x_ref[:, lanes].astype(F32)
        plain_grad = dot(b_ref[...], lam_low[:, lanes])
        weight_terms.append((x * plain_grad).astype(BF16))
        from_grad = weight * plain_grad
        dx_ref[:, lanes] = (dxmix_ref[:, lanes].astype(F32) + from_grad).astype(BF16)
        x_weighted.append((weight * x).astype(BF16))
    dc_ref[...] += dot_nt(jnp.concatenate(g_scaled, axis=1), h_low)
    db_ref[...] += dot_nt(jnp.concatenate(x_weighted, axis=1), lam_low)
    gather = gather_heads(step * (FINISH_LANES // DIM), FINISH_LANES, FINISH_LANES)
    none = jnp.zeros_like(gather)
    terms = dot(jnp.concatenate(start_terms, axis=1), jnp.concatenate([gather, none], axis=1))
    terms += dot(jnp.concatenate(weight_terms, axis=1), jnp.concatenate([none, gather], axis=1))
    terms_ref[...] += terms

    @pl.when(step == WIDTH // FINISH_LANES - 1)
    def _():
        end, weight, start = (scal_ref[k] for k in range(3))
        all_terms = terms_ref[...].T
        d_weight = all_terms[HEADS:]
        used = d_weight * weight
        d_cum = cpart_ref[...] + all_terms[:HEADS] - used
        d_total = jnp.sum(used, axis=1, keepdims=True)
        d_total = d_total + ddecay_ref[:, :1] * start[:, BLOCK - 1 :]
        square = (BLOCK, BLOCK)
        onward = ones_where(iota(square, 0) >= iota(square, 1))
        logs = dot(jnp.concatenate(split3(d_cum), axis=0), onward)
        d_log = logs[:HEADS] + logs[HEADS : 2 * HEADS] + logs[2 * HEADS :] + d_total
        d_dt = ddt_ref[...] + d_weight * end - rate_ref[:, :1] * d_log
        raw = raw_ref[...].astype(F32)
        raw_grad_ref[...] = (d_dt / (1.0 + jnp.exp(-raw))).astype(BF16)


def finish(
    x, g, ymix, dxmix, state, b, c, half, dbmix, dcmix, raw_t, rate, scal, cpart, ddecay, ddt
):
    lanes = FINISH_LANES
    return pl.pallas_call(
        finish_kernel,
        grid=(WIDTH // lanes,),
        in_specs=[
            wide(lanes), wide(lanes), wide(lanes), wide(lanes), pieces(lanes, CARRY),
            whole(BLOCK, STATE), whole(BLOCK, STATE),
            whole(5, BLOCK, 2 * HEADS), whole(BLOCK, STATE), whole(BLOCK, STATE),
            whole(HEADS, BLOCK), whole(HEADS, 128), whole(4, HEADS, BLOCK),
            whole(HEADS, BLOCK), whole(HEADS, 128), whole(HEADS, BLOCK),
        ],
        out_specs=[
            wide(lanes), wide(lanes), whole(BLOCK, STATE), whole(BLOCK, STATE),
            whole(HEADS, BLOCK),
        ],
        out_shape=[
            like((BLOCK, WIDTH), BF16), like((BLOCK, WIDTH), BF16),
            like((BLOCK, STATE)), like((BLOCK, STATE)), like((HEADS, BLOCK), BF16),
        ],
        scratch_shapes=[pltpu.VMEM((BLOCK, 2 * HEADS), F32)],
        compiler_params=params(),
        cost_estimate=cost(8 * 10**9, 16 * 10**6, 10**5),
        name="finish",
    )(x, g, ymix, dxmix, state, b, c, half, dbmix, dcmix, raw_t, rate, scal, cpart, ddecay, ddt)


def body(inputs, dt_raw, b_proj, c_proj, a_log, d_skip, seg_ids, cotangent):
    everyone = ("seq", "head")
    mine = lax.axis_index("head")
    place = mine.astype(jnp.int32).reshape(1)
    group = a_log.shape[0]
    gains = lax.all_gather(jnp.stack([a_log, d_skip]), "head", tiled=True)
    raw_t = dt_raw.T
    pay, scal, cum2, half, rate, seg, skip = states(
        place, raw_t, gains, seg_ids.reshape(-1, 128), inputs, cotangent, b_proj, c_proj
    )
    pay = lax.all_to_all(pay, everyone, 0, 0, tiled=True)
    ymix, dxmix, cpart, ddt, dbmix, dcmix, dskip, start_mom, end_mom = mix(
        inputs, cotangent, b_proj, c_proj, seg, skip, cum2, half
    )
    state = lax.all_to_all(scan(pay), everyone, 0, 0, tiled=True)
    ddecay, sums = gradient_sums(start_mom, end_mom, state, scal, cpart, dskip)
    sums = lax.all_to_all(sums.reshape(PARTS, 1, 128), everyone, 0, 0, tiled=True)
    y, dx, db, dc, raw_grad = finish(
        inputs, cotangent, ymix, dxmix, state, b_proj, c_proj, half, dbmix, dcmix,
        raw_t, rate, scal, cpart, ddecay, ddt,
    )
    sums = jnp.sum(sums, axis=(0, 1))
    a_grad = lax.dynamic_slice(sums, (mine * group,), (group,))
    skip_grad = lax.dynamic_slice(sums, (HEADS + mine * group,), (group,))
    return (y, dx, raw_grad.T, db, dc, a_grad, skip_grad)


def solution(mesh):
    tokens = P(("seq", "head"), None)
    in_specs = (tokens, tokens, tokens, tokens, P("head"), P("head"), P("seq"), tokens)
    out_specs = (tokens, tokens, tokens, tokens, tokens, P("head"), P("head"))
    return jax.shard_map(body, mesh=mesh, in_specs=in_specs, out_specs=out_specs, check_vma=False)
```
